256 devices in a mesh: outer: 16 (over x_hi, z), inner: 16 (over y, x_lo, core).
Axes of the slice: x: 4 (x_hi: 2, x_lo: 2; x = x_hi * 2 + x_lo), y: 4, z: 8, core: 2. Of those that a mesh axis runs over, the one named last changes fastest.
Arguments:
- activations: bfloat16 [65536, 8192], P(('outer', 'inner')), may hold values from -24 to 24
- output_grads: bfloat16 [65536, 512], P(('outer', 'inner')), may hold values from -0.0234375 to 0.0234375
- master_weights: float32 [8192, 512], P(('inner', 'outer')), may hold values from -0.0625 to 0.0625
- first_moment: float32 [8192, 512], P(('inner', 'outer')), may hold values from -5 to 5
- second_moment: float32 [8192, 512], P(('inner', 'outer')), may hold values from 0.1 to 2
- next_tokens: bfloat16 [65536, 8192], P(('outer', 'inner')), may hold values from -6 to 6
Outputs:
- new_master: float32 [8192, 512], P(('inner', 'outer'))
- new_first_moment: float32 [8192, 512], P(('inner', 'outer'))
- new_second_moment: float32 [8192, 512], P(('inner', 'outer'))
- kept_weights: bfloat16 [8192, 512], P('inner')
- projection: bfloat16 [65536, 512], P(('outer', 'inner'))
The draws below stay inside these ranges and needn't reach their ends.
All inputs are finite; a program needn't handle non-finite values.
Results may differ from the reference program's by a relative error of at most 0.012.
Values may be sent and summed in bfloat16 or wider, within the bound.
No kernel may reach another device: no remote copies, remote signals or barrier semaphores. Data moves between devices by JAX's collectives and lax.ppermute only.
A program may use at most 128 MiB of HBM per device.

```python
import math
import jax
import jax.numpy as jnp
from jax import lax

D = 8192
TOK_DEV = 256
ADAM_STEP = 10
KEY_COLS = 512
TOKENS = 65536


def raised(entries, stream_key, source, target, blocks, factor):
    def block_of(position):
        return (jnp.arange(entries.shape[position]) // (entries.shape[position] // blocks)).reshape((-1,) + (1,) * (entries.ndim - 1 - position))

    near = jax.random.permutation(stream_key, blocks)[block_of(target)]
    second = (block_of(target) + blocks // 2) % blocks
    return jnp.where((block_of(source) == near) | (block_of(source) == second), factor * entries, entries)


def levels(stream_key, extent, pieces, smallest, largest):
    level, own = 1.0, jax.random.fold_in(stream_key, 6)
    for axis_at, blocks in pieces:
        heights = jnp.exp(jax.random.uniform(jax.random.fold_in(own, axis_at), (blocks,), jnp.float32, smallest / len(pieces), largest / len(pieces)))
        level = level * jnp.repeat(heights, extent[axis_at] // blocks).reshape([-1 if axis == axis_at else 1 for axis in range(len(extent))])
    return level


def bell_draw(stream_key, extent, spread, most, split=(), dtype=jnp.bfloat16):
    array = jax.random.normal(stream_key, extent, jnp.float32) * spread
    if len(split) > 0:
        array = levels(stream_key, extent, split, -0.22, 0.18) * array
    return jnp.clip(array, min=-most, max=most).astype(dtype)


def heavy_noise(key, extent, deviation, reach, split, heavy, kind=jnp.bfloat16):
    drawn = deviation * jax.random.normal(key, extent, jnp.float32)
    if split:
        drawn = drawn * levels(key, extent, split, -0.22, 0.18)
    return jnp.clip(raised(drawn, jax.random.fold_in(key, 3), *heavy), -reach, reach).astype(kind)


def setup_inputs(seed: int = 0) -> dict:
    key_of = jax.random.split(jax.random.key(seed), 7)
    return {
        "activations": heavy_noise(key_of[0], (TOKENS, D), 1.0, 24.0, ((0, 256),), (0, 1, 256, 6.0)),
        "output_grads": bell_draw(key_of[1], (TOKENS, KEY_COLS), (TOKENS ** -0.5), 0.0234375, ((0, 256),)),
        "master_weights": bell_draw(key_of[2], (D, KEY_COLS), D ** -0.5, 0.0625, ((0, 256),), jnp.float32),
        "first_moment": bell_draw(key_of[3], (D, KEY_COLS), 1.0, 5.0, ((0, 256),), jnp.float32),
        "second_moment": jnp.clip(jnp.exp(math.log(2.0) - 2.9957323 * jax.random.uniform(key_of[4], (D, KEY_COLS), jnp.float32) ** levels(key_of[4], (D, KEY_COLS), ((0, 256),), -0.2, 0.2)), 0.1, 2.0),
        "next_tokens": bell_draw(key_of[5], (TOKENS, D), 1.0, 6.0, ((0, 256),)),
    }


beta_first = 0.9
beta_second = 0.95
learn_rate = 0.002
decay_rate = 0.1
adam_eps = 1e-08

def adamw_update(gradient, master_weights, first_moment, second_moment):
    new_first = beta_first * first_moment + (1.0 - beta_first) * gradient
    new_second = beta_second * second_moment + (1.0 - beta_second) * gradient * gradient
    first_hat = new_first / (1.0 - beta_first ** ADAM_STEP)
    second_hat = new_second / (1.0 - beta_second ** ADAM_STEP)
    new_master = master_weights - learn_rate * (first_hat / (jnp.sqrt(second_hat) + adam_eps) + decay_rate * master_weights)
    return (new_master, new_first, new_second)

def reference(activations, output_grads, master_weights, first_moment, second_moment, next_tokens):
    block_count = TOKENS // TOK_DEV
    act_blocks = activations.reshape(block_count, TOK_DEV, D)
    grad_blocks = output_grads.reshape(block_count, TOK_DEV, KEY_COLS)

    def accumulate(running, inputs):
        block_act, block_grad = inputs
        contrib = jnp.einsum('tr,tc->rc', block_act, block_grad, preferred_element_type=jnp.float32).astype(jnp.bfloat16)
        contrib = lax.optimization_barrier(contrib)
        return (running + contrib.astype(jnp.float32), None)
    gradient, _ = lax.scan(accumulate, jnp.zeros((D, KEY_COLS), jnp.float32), (act_blocks, grad_blocks))
    new_master, new_first, new_second = adamw_update(gradient, master_weights, first_moment, second_moment)
    kept_weights = new_master.astype(jnp.bfloat16)
    projection = jnp.dot(next_tokens, kept_weights, preferred_element_type=jnp.float32).astype(jnp.bfloat16)
    return (new_master, new_first, new_second, kept_weights, projection)
```

```python
import itertools

import jax
import jax.numpy as jnp
from jax import lax
from jax.experimental import pallas as pl
from jax.experimental.pallas import tpu as pltpu
from jax.sharding import PartitionSpec as P

ADAM_STEP = 10
beta_first = 0.9
beta_second = 0.95
learn_rate = 0.002
decay_rate = 0.1
adam_eps = 1e-08

AXES = ("outer", "inner")
SIZES = (2, 8, 4, 2, 2)
TOK = 256
COLS = 512
WIDTH = 8192
HALF = WIDTH // 2
PARTS = 4
BLOCKS = 16
ROWS = 64

ORDERS = ((0, 2, 1, 3), (1, 3, 0, 2), (2, 0, 3, 1), (3, 1, 2, 0))
Z_STEPS = (1, 2, 4)


def moves(change):
    pairs = []
    for here in itertools.product(*(range(n) for n in SIZES)):
        source = target = 0
        for n, i, j in zip(SIZES, here, change(*here)):
            source, target = source * n + i, target * n + j
        pairs.append((source, target))
    return pairs


def pair_x(odd):
    def change(xh, z, y, xl, c):
        x = xh * 2 + xl
        x = ((x ^ 1) if not odd else ((x + 1) % 4 if x % 2 else (x - 1) % 4))
        return x // 2, z, y, x % 2, c

    return change


def pair_y(odd):
    def change(xh, z, y, xl, c):
        y = (y ^ 1) if not odd else ((y + 1) % 4 if y % 2 else (y - 1) % 4)
        return xh, z, y, xl, c

    return change


PAIRINGS = (moves(pair_x(0)), moves(pair_x(1)), moves(pair_y(0)), moves(pair_y(1)))


def across(array, pairing):
    return lax.ppermute(array, AXES, PAIRINGS[pairing])


def z_swap(array, mask):
    return lax.ppermute(array, AXES, moves(lambda xh, z, y, xl, c: (xh, z ^ mask, y, xl, c)))


def core_swap(array):
    return lax.ppermute(array, AXES, moves(lambda xh, z, y, xl, c: (xh, z, y, xl, 1 - c)))


def place():
    outer, inner = lax.axis_index("outer"), lax.axis_index("inner")
    xh, z = outer // 8, outer % 8
    y, xl, c = inner // 4, (inner // 2) % 2, inner % 2
    return xh, z, y, xl, c


def block_table(xh, y, xl, core):
    r = jnp.arange(BLOCKS, dtype=jnp.int32)
    a, b, c, d = (r >> 3) & 1, (r >> 2) & 1, (r >> 1) & 1, r & 1
    to_xh, to_xl = xh ^ b, xl ^ a ^ b
    to_y = y ^ (2 * d) ^ (c ^ d)
    return ((to_y * 2 + to_xl) * 2 + core) * 2 + to_xh


def pack_kernel(table, source, packed):
    packed[...] = source[...]


def pack(array, table):
    return pl.pallas_call(
        pack_kernel,
        out_shape=jax.ShapeDtypeStruct((TOK, HALF), jnp.bfloat16),
        grid_spec=pltpu.PrefetchScalarGridSpec(
            num_scalar_prefetch=1,
            grid=(BLOCKS,),
            in_specs=[pl.BlockSpec((TOK, 256), lambda r, t: (0, t[r]))],
            out_specs=pl.BlockSpec((TOK, 256), lambda r, t: (0, r)),
        ),
        name="pack",
    )(table, array)


def term_kernel(table, own, other, grads_own, grads_other, term):
    dims = (((0,), (0,)), ((), ()))
    total = lax.dot_general(own[...], grads_own[...], dims, preferred_element_type=jnp.float32)
    total += lax.dot_general(other[...], grads_other[...], dims, preferred_element_type=jnp.float32)
    term[...] = total.astype(jnp.bfloat16).reshape(term.shape)


def gradient_term(table, own, other, grads_own, grads_other):
    whole = pl.BlockSpec((TOK, COLS), lambda r, t: (0, 0))
    return pl.pallas_call(
        term_kernel,
        out_shape=jax.ShapeDtypeStruct((PARTS, BLOCKS, ROWS, COLS), jnp.bfloat16),
        grid_spec=pltpu.PrefetchScalarGridSpec(
            num_scalar_prefetch=1,
            grid=(BLOCKS,),
            in_specs=[
                pl.BlockSpec((TOK, 256), lambda r, t: (0, t[r])),
                pl.BlockSpec((TOK, 256), lambda r, t: (0, r)),
                whole,
                whole,
            ],
            out_specs=pl.BlockSpec((PARTS, 1, ROWS, COLS), lambda r, t: (0, r, 0, 0)),
        ),
        name="gradient_term",
    )(table, own, other, grads_own, grads_other)


def project_kernel(table, own, other, *refs):
    parts, (mine, theirs, total_mine, total_theirs) = refs[:PARTS], refs[PARTS:]
    step = pl.program_id(0)

    @pl.when(step == 0)
    def _():
        total_mine[...] = jnp.zeros_like(total_mine)
        total_theirs[...] = jnp.zeros_like(total_theirs)

    weights = jnp.concatenate([p[...].reshape(ROWS, COLS) for p in parts], axis=0)
    total_mine[...] += jnp.dot(own[...], weights, preferred_element_type=jnp.float32)
    total_theirs[...] += jnp.dot(other[...], weights, preferred_element_type=jnp.float32)

    @pl.when(step == BLOCKS - 1)
    def _():
        mine[...] = total_mine[...]
        theirs[...] = total_theirs[...]


def project(table, own, other, parts):
    out = pl.BlockSpec((TOK, COLS), lambda r, t: (0, 0))
    shape = jax.ShapeDtypeStruct((TOK, COLS), jnp.float32)
    return pl.pallas_call(
        project_kernel,
        out_shape=(shape, shape),
        grid_spec=pltpu.PrefetchScalarGridSpec(
            num_scalar_prefetch=1,
            grid=(BLOCKS,),
            in_specs=[
                pl.BlockSpec((TOK, 256), lambda r, t: (0, t[r])),
                pl.BlockSpec((TOK, 256), lambda r, t: (0, r)),
            ]
            + [pl.BlockSpec((1, ROWS, COLS), lambda r, t: (r, 0, 0))] * PARTS,
            out_specs=(out, out),
            scratch_shapes=[pltpu.VMEM((TOK, COLS), jnp.float32)] * 2,
        ),
        name="project",
    )(table, own, other, *parts)


def adamw_update(gradient, master_weights, first_moment, second_moment):
    new_first = beta_first * first_moment + (1.0 - beta_first) * gradient
    new_second = beta_second * second_moment + (1.0 - beta_second) * gradient * gradient
    first_hat = new_first / (1.0 - beta_first**ADAM_STEP)
    second_hat = new_second / (1.0 - beta_second**ADAM_STEP)
    new_master = master_weights - learn_rate * (
        first_hat / (jnp.sqrt(second_hat) + adam_eps) + decay_rate * master_weights
    )
    return (new_master, new_first, new_second)


def wide(array):
    return array.astype(jnp.float32)


def half_of(array, dim, index):
    return lax.index_in_dim(array, index, dim, keepdims=True)


def reduce_parts(term):
    parts = [term[i].reshape(2, 2, 2, 2, ROWS, COLS) for i in range(PARTS)]
    for step in range(4):
        later = []
        for i in range(PARTS):
            v = ORDERS[i][step]
            got = across(half_of(parts[i], v, 1), v)
            later.append((wide(half_of(parts[i], v, 0)) + wide(got)).astype(jnp.bfloat16))
        parts = later
    return jnp.concatenate([p.reshape(ROWS, COLS) for p in parts], axis=0)


def reduce_z(rows, z):
    total = rows.reshape(2, 2, 2, 32, COLS)
    for mask, bit_dim in ((1, 2), (2, 1), (4, 0)):
        bit = (z & mask) != 0
        low, high = half_of(total, bit_dim, 0), half_of(total, bit_dim, 1)
        got = z_swap(jnp.where(bit, low, high), mask)
        total = wide(jnp.where(bit, high, low)) + wide(got)
        if mask != 4:
            total = total.astype(jnp.bfloat16)
    return total.reshape(32, COLS)


def gather_z(shard, z):
    rows = shard[None]
    for mask in (4, 2, 1):
        got = z_swap(rows, mask)
        bit = (z & mask) != 0
        rows = jnp.stack([jnp.where(bit, got, rows), jnp.where(bit, rows, got)], axis=1)
        rows = rows.reshape(-1, 32, COLS)
    return rows.reshape(2, 2, 2, 32, COLS)


def gather_parts(rows):
    parts = [rows[i * ROWS : (i + 1) * ROWS].reshape(1, 1, 1, 1, ROWS, COLS) for i in range(PARTS)]
    for step in range(4):
        later = []
        for i in range(PARTS):
            v = ORDERS[i][3 - step]
            got = across(parts[i], v)
            later.append(jnp.concatenate([parts[i], got], axis=v))
        parts = later
    return [p.reshape(BLOCKS, ROWS, COLS) for p in parts]


def local(activations, output_grads, master_weights, first_moment, second_moment, next_tokens):
    xh, z, y, xl, core = place()
    table = block_table(xh, y, xl, core)
    other_table = block_table(xh, y, xl, 1 - core)

    got_acts = core_swap(pack(activations, other_table))
    got_grads = core_swap(output_grads)
    got_tokens = core_swap(pack(next_tokens, other_table))

    term = gradient_term(table, activations, got_acts, output_grads, got_grads)
    gradient = reduce_z(reduce_parts(term), z)
    new_master, new_first, new_second = adamw_update(
        gradient, master_weights, first_moment, second_moment
    )
    rows = gather_z(new_master.astype(jnp.bfloat16), z).reshape(256, COLS)
    parts = gather_parts(rows)

    far = jnp.concatenate([p[12] for p in parts], axis=0)
    low = xh == 0
    kept_weights = jnp.concatenate([jnp.where(low, rows, far), jnp.where(low, far, rows)], axis=0)

    mine, theirs = project(table, next_tokens, got_tokens, parts)
    projection = (mine + core_swap(theirs)).astype(jnp.bfloat16)
    return (new_master, new_first, new_second, kept_weights, projection)


def solution(mesh):
    placed = (
        P(("outer", "inner"), None),
        P(("outer", "inner"), None),
        P(("inner", "outer"), None),
        P(("inner", "outer"), None),
        P(("inner", "outer"), None),
        P(("outer", "inner"), None),
    )
    return jax.shard_map(
        local,
        mesh=mesh,
        in_specs=placed,
        out_specs=(
            P(("inner", "outer"), None),
            P(("inner", "outer"), None),
            P(("inner", "outer"), None),
            P("inner", None),
            P(("outer", "inner"), None),
        ),
        check_vma=False,
    )
```

```python
import functools
import itertools

import jax
import jax.numpy as jnp
from jax import lax
from jax.experimental import pallas as pl
from jax.experimental.pallas import tpu as pltpu
from jax.sharding import PartitionSpec as P

ADAM_STEP = 10
beta_first = 0.9
beta_second = 0.95
learn_rate = 0.002
decay_rate = 0.1
adam_eps = 1e-08

AXES = ("outer", "inner")
SIZES = (2, 8, 4, 2, 2)
TOK = 256
COLS = 512
HALF = 4096
BLOCK = 256
BLOCKS = 16
PARTS = 4
ROWS = 64

ORDERS = ((0, 2, 1, 3), (1, 3, 0, 2), (2, 0, 3, 1), (3, 1, 2, 0))


def moves(change):
    pairs = []
    for here in itertools.product(*(range(n) for n in SIZES)):
        source = target = 0
        for n, i, j in zip(SIZES, here, change(*here)):
            source, target = source * n + i, target * n + j
        pairs.append((source, target))
    return pairs


def paired(i, odd):
    if odd:
        return (i + 1) % 4 if i % 2 else (i - 1) % 4
    return i ^ 1


def pair_x(odd, xh, z, y, xl, c):
    x = paired(xh * 2 + xl, odd)
    return x // 2, z, y, x % 2, c


def pair_y(odd, xh, z, y, xl, c):
    return xh, z, paired(y, odd), xl, c


PAIRINGS = tuple(moves(functools.partial(f, odd)) for f in (pair_x, pair_y) for odd in (0, 1))


def across(array, pairing):
    return lax.ppermute(array, AXES, PAIRINGS[pairing])


def z_swap(array, mask):
    return lax.ppermute(array, AXES, moves(lambda xh, z, y, xl, c: (xh, z ^ mask, y, xl, c)))


def core_swap(array):
    return lax.ppermute(array, AXES, moves(lambda xh, z, y, xl, c: (xh, z, y, xl, 1 - c)))


def place():
    outer, inner = lax.axis_index("outer"), lax.axis_index("inner")
    return outer // 8, outer % 8, inner // 4, (inner // 2) % 2, inner % 2


def columns_of(where, r, core):
    xh, _, y, xl, _ = where
    a, b, c, d = (r >> 3) & 1, (r >> 2) & 1, (r >> 1) & 1, r & 1
    to_xh, to_xl, to_y = xh ^ b, xl ^ (a ^ b), y ^ (2 * d + (c ^ d))
    block = ((to_y * 2 + to_xl) * 2 + core) * 2 + to_xh
    return pl.ds(pl.multiple_of(block * BLOCK, BLOCK), BLOCK)


def side_and_slot(m, r):
    bits = [(r >> (3 - v)) & 1 for v in range(4)]
    side = bits.pop(ORDERS[m][0])
    return side, bits[0] * 4 + bits[1] * 2 + bits[2]


def pair_rows(where, m):
    z = where[1]
    first = jnp.where(z < 4, z, 7 - z) ^ m
    return (
        pl.ds(pl.multiple_of(first * 32, 32), 32),
        pl.ds(pl.multiple_of((7 - first) * 32, 32), 32),
    )


ANY = pl.BlockSpec(memory_space=pl.ANY)
VMEM = pl.BlockSpec(memory_space=pltpu.VMEM)
PARAMS = pltpu.CompilerParams(vmem_limit_bytes=40 * 1024 * 1024)


def pack_kernel(acts, master, first, second, packed, state, sems):
    where = place()
    copies = [
        pltpu.make_async_copy(
            acts.at[:, columns_of(where, r, 1 - where[4])],
            packed.at[:, pl.ds(r * BLOCK, BLOCK)],
            sems.at[r],
        )
        for r in range(BLOCKS)
    ] + [
        pltpu.make_async_copy(source, state.at[i], sems.at[BLOCKS + i])
        for i, source in enumerate((master, first, second))
    ]
    for copy in copies:
        copy.start()
    for copy in copies:
        copy.wait()


def pack(acts, master, first, second):
    return pl.pallas_call(
        pack_kernel,
        out_shape=(
            jax.ShapeDtypeStruct((TOK, HALF), jnp.bfloat16),
            jax.ShapeDtypeStruct((3, 32, COLS), jnp.float32),
        ),
        in_specs=[ANY] * 4,
        out_specs=(ANY, ANY),
        scratch_shapes=[pltpu.SemaphoreType.DMA((BLOCKS + 3,))],
        compiler_params=PARAMS,
        name="pack",
    )(acts, master, first, second)


def term_kernel(acts, got, grads, got_grads, tokens, *refs):
    halves, packed, both, grads_both, term, sems = (
        refs[: 2 * PARTS],
        *refs[2 * PARTS :],
    )
    where = place()
    own, other, pack_copies = [], [], []
    for r in range(BLOCKS):
        here = pl.ds(r * BLOCK, BLOCK)
        own.append(
            pltpu.make_async_copy(
                acts.at[:, columns_of(where, r, where[4])], both.at[:TOK, here], sems.at[r]
            )
        )
        other.append(
            pltpu.make_async_copy(got.at[:, here], both.at[TOK:, here], sems.at[BLOCKS + r])
        )
        pack_copies.append(
            pltpu.make_async_copy(
                tokens.at[:, columns_of(where, r, 1 - where[4])],
                packed.at[:, here],
                sems.at[2 * BLOCKS + r],
            )
        )
    for r in range(BLOCKS):
        own[r].start()
        other[r].start()
    grads_both[:TOK] = grads[...]
    grads_both[TOK:] = got_grads[...]
    rows = [pair_rows(where, m) for m in range(PARTS)]
    for r in range(BLOCKS):
        own[r].wait()
        other[r].wait()
        pack_copies[r].start()
        term[r % 2] = lax.dot_general(
            both[:, r * BLOCK : (r + 1) * BLOCK],
            grads_both[...],
            (((0,), (0,)), ((), ())),
            preferred_element_type=jnp.float32,
        ).astype(jnp.bfloat16)
        for m in range(PARTS):
            side, slot = side_and_slot(m, r)
            out = halves[2 * m + side]
            out[slot, :32] = term[r % 2, rows[m][0]]
            out[slot, 32:] = term[r % 2, rows[m][1]]
    for copy in pack_copies:
        copy.wait()


def gradient_term(acts, got, grads, got_grads, tokens):
    half = jax.ShapeDtypeStruct((8, ROWS, COLS), jnp.bfloat16)
    return pl.pallas_call(
        term_kernel,
        out_shape=(half,) * (2 * PARTS) + (jax.ShapeDtypeStruct((TOK, HALF), jnp.bfloat16),),
        in_specs=[ANY, ANY, VMEM, VMEM, ANY],
        out_specs=(VMEM,) * (2 * PARTS) + (ANY,),
        scratch_shapes=[
            pltpu.VMEM((2 * TOK, HALF), jnp.bfloat16),
            pltpu.VMEM((2 * TOK, COLS), jnp.bfloat16),
            pltpu.VMEM((2, BLOCK, COLS), jnp.bfloat16),
            pltpu.SemaphoreType.DMA((3 * BLOCKS,)),
        ],
        compiler_params=PARAMS,
        name="gradient_term",
    )(acts, got, grads, got_grads, tokens)


STRIPE = 1024


def project_kernel(tokens, got, *refs):
    halves = refs[: 2 * PARTS]
    kept, mine, theirs, both, held, weights, total, sems = refs[2 * PARTS :]
    where = place()
    weight_copies = [
        pltpu.make_async_copy(halves[i], held.at[i], sems.at[i]) for i in range(2 * PARTS)
    ]
    token_copies = [
        pltpu.make_async_copy(
            tokens.at[:, columns_of(where, r, where[4])],
            both.at[:TOK, pl.ds(r * BLOCK, BLOCK)],
            sems.at[8 + r],
        )
        for r in range(BLOCKS)
    ]
    got_copies = [
        pltpu.make_async_copy(
            got.at[:, pl.ds(s * STRIPE, STRIPE)],
            both.at[TOK:, pl.ds(s * STRIPE, STRIPE)],
            sems.at[8 + BLOCKS + s],
        )
        for s in range(HALF // STRIPE)
    ]
    for copy in weight_copies + token_copies + got_copies:
        copy.start()
    rows = [pair_rows(where, m) for m in range(PARTS)]
    for copy in weight_copies:
        copy.wait()
    per = STRIPE // BLOCK
    for s in range(HALF // STRIPE):
        for k in range(per):
            r = s * per + k
            for m in range(PARTS):
                side, slot = side_and_slot(m, r)
                for j in range(2):
                    at = pl.ds(pl.multiple_of(k * BLOCK + rows[m][j].start, 32), 32)
                    weights[s % 2, at] = held[2 * m + side, slot, j * 32 : j * 32 + 32]
            token_copies[r].wait()
        got_copies[s].wait()
        if s == 0:
            kept[pl.ds(pl.multiple_of(where[0] * BLOCK, BLOCK), BLOCK)] = weights[0, :BLOCK]
        if s == 3:
            kept[pl.ds(pl.multiple_of((1 - where[0]) * BLOCK, BLOCK), BLOCK)] = weights[1, :BLOCK]
        product = jnp.dot(
            both[:, s * STRIPE : (s + 1) * STRIPE],
            weights[s % 2],
            preferred_element_type=jnp.float32,
        )
        if s == 0:
            total[...] = product
        elif s < HALF // STRIPE - 1:
            total[...] += product
        else:
            product += total[...]
            mine[...] = product[:TOK]
            theirs[...] = product[TOK:].astype(jnp.bfloat16)


def project(tokens, got, halves):
    return pl.pallas_call(
        project_kernel,
        out_shape=(
            jax.ShapeDtypeStruct((2 * BLOCK, COLS), jnp.bfloat16),
            jax.ShapeDtypeStruct((TOK, COLS), jnp.float32),
            jax.ShapeDtypeStruct((TOK, COLS), jnp.bfloat16),
        ),
        in_specs=[ANY] * (2 + 2 * PARTS),
        out_specs=(VMEM,) * 3,
        scratch_shapes=[
            pltpu.VMEM((2 * TOK, HALF), jnp.bfloat16),
            pltpu.VMEM((2 * PARTS, 8, ROWS, COLS), jnp.bfloat16),
            pltpu.VMEM((2, STRIPE, COLS), jnp.bfloat16),
            pltpu.VMEM((2 * TOK, COLS), jnp.float32),
            pltpu.SemaphoreType.DMA((8 + BLOCKS + HALF // STRIPE,)),
        ],
        compiler_params=PARAMS,
        name="project",
    )(tokens, got, *halves)


def adamw_update(gradient, master_weights, first_moment, second_moment):
    new_first = beta_first * first_moment + (1.0 - beta_first) * gradient
    new_second = beta_second * second_moment + (1.0 - beta_second) * gradient * gradient
    first_hat = new_first / (1.0 - beta_first**ADAM_STEP)
    second_hat = new_second / (1.0 - beta_second**ADAM_STEP)
    new_master = master_weights - learn_rate * (
        first_hat / (jnp.sqrt(second_hat) + adam_eps) + decay_rate * master_weights
    )
    return (new_master, new_first, new_second)


def wide(array):
    return array.astype(jnp.float32)


def reduce_parts(halves):
    parts = []
    left = []
    for m in range(PARTS):
        keep, send = halves[2 * m], halves[2 * m + 1]
        left.append([v for v in range(4) if v != ORDERS[m][0]])
        got = across(send, ORDERS[m][0])
        parts.append((wide(keep) + wide(got)).astype(jnp.bfloat16).reshape(2, 2, 2, ROWS, COLS))
    for step in range(1, 4):
        for m in range(PARTS):
            v = ORDERS[m][step]
            dim = left[m].index(v)
            left[m].remove(v)
            keep = lax.index_in_dim(parts[m], 0, dim, keepdims=False)
            got = across(lax.index_in_dim(parts[m], 1, dim, keepdims=False), v)
            total = wide(keep) + wide(got)
            parts[m] = total if step == 3 and m == 0 else total.astype(jnp.bfloat16)
    return parts


def reduce_z(parts):
    total = parts[0]
    for m in range(1, PARTS):
        total = total + wide(z_swap(parts[m], m))
    total = total.astype(jnp.bfloat16)
    return (wide(total) + wide(z_swap(total, 7))).reshape(2, 32, COLS)


def gather_parts(pair):
    parts = [pair] + [z_swap(pair, m) for m in range(1, PARTS)]
    known = [[] for _ in range(PARTS)]
    for step in range(3, 0, -1):
        for m in range(PARTS):
            v = ORDERS[m][step]
            known[m] = sorted(known[m] + [v])
            parts[m] = jnp.stack([parts[m], across(parts[m], v)], axis=known[m].index(v))
    halves = []
    for m in range(PARTS):
        keep = parts[m].reshape(8, ROWS, COLS)
        halves += [keep, across(keep, ORDERS[m][0])]
    return halves


def local(activations, output_grads, master_weights, first_moment, second_moment, next_tokens):
    low = lax.axis_index("outer") % 8 < 4
    packed, state = pack(activations, master_weights, first_moment, second_moment)
    got_acts = core_swap(packed)
    got_grads = core_swap(output_grads)
    got_state = z_swap(state, 7)
    *halves, packed_tokens = gradient_term(
        activations, got_acts, output_grads, got_grads, next_tokens
    )
    got_tokens = core_swap(packed_tokens)

    gradient = reduce_z(reduce_parts(halves))
    pairs = jnp.stack([jnp.where(low, state, got_state), jnp.where(low, got_state, state)], axis=1)
    updated = adamw_update(gradient, *pairs)
    new_master, new_first, new_second = (jnp.where(low, u[0], u[1]) for u in updated)
    pair = updated[0].astype(jnp.bfloat16).reshape(ROWS, COLS)

    kept_weights, mine, theirs = project(next_tokens, got_tokens, gather_parts(pair))
    projection = (mine + wide(core_swap(theirs))).astype(jnp.bfloat16)
    return (new_master, new_first, new_second, kept_weights, projection)


def solution(mesh):
    placed = (
        P(("outer", "inner"), None),
        P(("outer", "inner"), None),
        P(("inner", "outer"), None),
        P(("inner", "outer"), None),
        P(("inner", "outer"), None),
        P(("outer", "inner"), None),
    )
    return jax.shard_map(
        local,
        mesh=mesh,
        in_specs=placed,
        out_specs=(
            P(("inner", "outer"), None),
            P(("inner", "outer"), None),
            P(("inner", "outer"), None),
            P("inner", None),
            P(("outer", "inner"), None),
        ),
        check_vma=False,
    )
```

```python
import functools
import itertools

import jax
import jax.numpy as jnp
from jax import lax
from jax.experimental import pallas as pl
from jax.experimental.pallas import tpu as pltpu
from jax.sharding import PartitionSpec as P

ADAM_STEP = 10
beta_first = 0.9
beta_second = 0.95
learn_rate = 0.002
decay_rate = 0.1
adam_eps = 1e-08

AXES = ("outer", "inner")
SIZES = (2, 8, 4, 2, 2)
TOK = 256
COLS = 512
HALF = 4096
BLOCK = 256
BLOCKS = 16
PARTS = 4
ROWS = 64

ORDERS = ((0, 2, 1, 3), (1, 3, 0, 2), (2, 0, 1, 3), (3, 1, 0, 2))
COUPLES = ((0, 2), (1, 3))


def moves(change):
    pairs = []
    for here in itertools.product(*(range(n) for n in SIZES)):
        source = target = 0
        for n, i, j in zip(SIZES, here, change(*here)):
            source, target = source * n + i, target * n + j
        pairs.append((source, target))
    return pairs


def paired(i, odd):
    if odd:
        return (i + 1) % 4 if i % 2 else (i - 1) % 4
    return i ^ 1


def pair_x(odd, xh, z, y, xl, c):
    x = paired(xh * 2 + xl, odd)
    return x // 2, z, y, x % 2, c


def pair_y(odd, xh, z, y, xl, c):
    return xh, z, paired(y, odd), xl, c


PAIRINGS = tuple(moves(functools.partial(f, odd)) for f in (pair_x, pair_y) for odd in (0, 1))


def across(array, pairing):
    return lax.ppermute(array, AXES, PAIRINGS[pairing])


def z_swap(array, mask):
    return lax.ppermute(array, AXES, moves(lambda xh, z, y, xl, c: (xh, z ^ mask, y, xl, c)))


def core_swap(array):
    return lax.ppermute(array, AXES, moves(lambda xh, z, y, xl, c: (xh, z, y, xl, 1 - c)))


def place():
    outer, inner = lax.axis_index("outer"), lax.axis_index("inner")
    return outer // 8, outer % 8, inner // 4, (inner // 2) % 2, inner % 2


def columns_of(where, r, core):
    xh, _, y, xl, _ = where
    a, b, c, d = (r >> 3) & 1, (r >> 2) & 1, (r >> 1) & 1, r & 1
    to_xh, to_xl, to_y = xh ^ b, xl ^ (a ^ b), y ^ (2 * d + (c ^ d))
    block = ((to_y * 2 + to_xl) * 2 + core) * 2 + to_xh
    return pl.ds(pl.multiple_of(block * BLOCK, BLOCK), BLOCK)


def side_and_slot(m, r):
    bits = [(r >> (3 - v)) & 1 for v in range(4)]
    side = bits.pop(ORDERS[m][0])
    return side, bits[0] * 4 + bits[1] * 2 + bits[2]


def pair_rows(where, m):
    z = where[1]
    first = jnp.where(z < 4, z, 7 - z) ^ m
    return (
        pl.ds(pl.multiple_of(first * 32, 32), 32),
        pl.ds(pl.multiple_of((7 - first) * 32, 32), 32),
    )


ANY = pl.BlockSpec(memory_space=pl.ANY)
HBM = pl.BlockSpec(memory_space=pltpu.HBM)
VMEM = pl.BlockSpec(memory_space=pltpu.VMEM)
PARAMS = pltpu.CompilerParams(vmem_limit_bytes=40 * 1024 * 1024)


def pack_kernel(acts, tokens, master, first, second, packed, packed_tokens, state, sems):
    where = place()
    copies = [
        pltpu.make_async_copy(
            source.at[:, columns_of(where, r, 1 - where[4])],
            target.at[:, pl.ds(r * BLOCK, BLOCK)],
            sems.at[i * BLOCKS + r],
        )
        for i, (source, target) in enumerate(((acts, packed), (tokens, packed_tokens)))
        for r in range(BLOCKS)
    ] + [
        pltpu.make_async_copy(source, state.at[i], sems.at[2 * BLOCKS + i])
        for i, source in enumerate((master, first, second))
    ]
    for copy in copies:
        copy.start()
    for copy in copies:
        copy.wait()


def pack(acts, tokens, master, first, second):
    half = jax.ShapeDtypeStruct((TOK, HALF), jnp.bfloat16)
    return pl.pallas_call(
        pack_kernel,
        out_shape=(half, half, jax.ShapeDtypeStruct((3, 32, COLS), jnp.float32)),
        in_specs=[HBM] * 5,
        out_specs=(ANY,) * 3,
        scratch_shapes=[pltpu.SemaphoreType.DMA((2 * BLOCKS + 3,))],
        compiler_params=PARAMS,
        name="pack",
    )(acts, tokens, master, first, second)


def term_kernel(acts, got, grads, got_grads, _tokens, _state, *refs):
    halves = refs[: 2 * PARTS]
    both, grads_both, term, sems = refs[2 * PARTS :]
    where = place()
    own, other = [], []
    for r in range(BLOCKS):
        here = pl.ds(r * BLOCK, BLOCK)
        own.append(
            pltpu.make_async_copy(
                acts.at[:, columns_of(where, r, where[4])], both.at[:TOK, here], sems.at[r]
            )
        )
        other.append(
            pltpu.make_async_copy(got.at[:, here], both.at[TOK:, here], sems.at[BLOCKS + r])
        )
    for r in range(BLOCKS):
        own[r].start()
        other[r].start()
    grads_both[:TOK] = grads[...]
    grads_both[TOK:] = got_grads[...]
    rows = [pair_rows(where, m) for m in range(PARTS)]
    for r in range(BLOCKS):
        own[r].wait()
        other[r].wait()
        term[r % 2] = lax.dot_general(
            both[:, r * BLOCK : (r + 1) * BLOCK],
            grads_both[...],
            (((0,), (0,)), ((), ())),
            preferred_element_type=jnp.float32,
        ).astype(jnp.bfloat16)
        for m in range(PARTS):
            side, slot = side_and_slot(m, r)
            out = halves[2 * m + side]
            out[slot, :32] = term[r % 2, rows[m][0]]
            out[slot, 32:] = term[r % 2, rows[m][1]]


def gradient_term(acts, got, grads, got_grads, got_tokens, got_state):
    half = jax.ShapeDtypeStruct((8, ROWS, COLS), jnp.bfloat16)
    return pl.pallas_call(
        term_kernel,
        out_shape=(half,) * (2 * PARTS),
        in_specs=[HBM, ANY, VMEM, VMEM, ANY, ANY],
        out_specs=(VMEM,) * (2 * PARTS),
        scratch_shapes=[
            pltpu.VMEM((2 * TOK, HALF), jnp.bfloat16),
            pltpu.VMEM((2 * TOK, COLS), jnp.bfloat16),
            pltpu.VMEM((2, BLOCK, COLS), jnp.bfloat16),
            pltpu.SemaphoreType.DMA((2 * BLOCKS,)),
        ],
        compiler_params=PARAMS,
        name="gradient_term",
    )(acts, got, grads, got_grads, got_tokens, got_state)


STRIPE = 1024


def project_kernel(tokens, got, *refs):
    halves = refs[: 2 * PARTS]
    kept, mine, theirs, both, held, weights, total, sems = refs[2 * PARTS :]
    where = place()
    weight_copies = [
        pltpu.make_async_copy(halves[i], held.at[i], sems.at[i]) for i in range(2 * PARTS)
    ]
    token_copies = [
        pltpu.make_async_copy(
            tokens.at[:, columns_of(where, r, where[4])],
            both.at[:TOK, pl.ds(r * BLOCK, BLOCK)],
            sems.at[8 + r],
        )
        for r in range(BLOCKS)
    ]
    got_copies = [
        pltpu.make_async_copy(
            got.at[:, pl.ds(s * STRIPE, STRIPE)],
            both.at[TOK:, pl.ds(s * STRIPE, STRIPE)],
            sems.at[8 + BLOCKS + s],
        )
        for s in range(HALF // STRIPE)
    ]
    for copy in weight_copies + token_copies + got_copies:
        copy.start()
    rows = [pair_rows(where, m) for m in range(PARTS)]
    for copy in weight_copies:
        copy.wait()
    per = STRIPE // BLOCK
    for s in range(HALF // STRIPE):
        for k in range(per):
            r = s * per + k
            for m in range(PARTS):
                side, slot = side_and_slot(m, r)
                for j in range(2):
                    at = pl.ds(pl.multiple_of(k * BLOCK + rows[m][j].start, 32), 32)
                    weights[s % 2, at] = held[2 * m + side, slot, j * 32 : j * 32 + 32]
            token_copies[r].wait()
        got_copies[s].wait()
        if s == 0:
            kept[pl.ds(pl.multiple_of(where[0] * BLOCK, BLOCK), BLOCK)] = weights[0, :BLOCK]
        if s == 3:
            kept[pl.ds(pl.multiple_of((1 - where[0]) * BLOCK, BLOCK), BLOCK)] = weights[1, :BLOCK]
        product = jnp.dot(
            both[:, s * STRIPE : (s + 1) * STRIPE],
            weights[s % 2],
            preferred_element_type=jnp.float32,
        )
        if s == 0:
            total[...] = product
        elif s < HALF // STRIPE - 1:
            total[...] += product
        else:
            product += total[...]
            mine[...] = product[:TOK]
            theirs[...] = product[TOK:].astype(jnp.bfloat16)


def project(tokens, got, halves):
    return pl.pallas_call(
        project_kernel,
        out_shape=(
            jax.ShapeDtypeStruct((2 * BLOCK, COLS), jnp.bfloat16),
            jax.ShapeDtypeStruct((TOK, COLS), jnp.float32),
            jax.ShapeDtypeStruct((TOK, COLS), jnp.bfloat16),
        ),
        in_specs=[HBM] + [ANY] * (1 + 2 * PARTS),
        out_specs=(VMEM,) * 3,
        scratch_shapes=[
            pltpu.VMEM((2 * TOK, HALF), jnp.bfloat16),
            pltpu.VMEM((2 * PARTS, 8, ROWS, COLS), jnp.bfloat16),
            pltpu.VMEM((2, STRIPE, COLS), jnp.bfloat16),
            pltpu.VMEM((2 * TOK, COLS), jnp.float32),
            pltpu.SemaphoreType.DMA((8 + BLOCKS + HALF // STRIPE,)),
        ],
        compiler_params=PARAMS,
        name="project",
    )(tokens, got, *halves)


def adamw_update(gradient, master_weights, first_moment, second_moment):
    new_first = beta_first * first_moment + (1.0 - beta_first) * gradient
    new_second = beta_second * second_moment + (1.0 - beta_second) * gradient * gradient
    first_hat = new_first / (1.0 - beta_first**ADAM_STEP)
    second_hat = new_second / (1.0 - beta_second**ADAM_STEP)
    new_master = master_weights - learn_rate * (
        first_hat / (jnp.sqrt(second_hat) + adam_eps) + decay_rate * master_weights
    )
    return (new_master, new_first, new_second)


def wide(array):
    return array.astype(jnp.float32)


def add(keep, got):
    return (wide(keep) + wide(got)).astype(jnp.bfloat16)


def halve(array, dim, pairing):
    keep = lax.index_in_dim(array, 0, dim, keepdims=False)
    return add(keep, across(lax.index_in_dim(array, 1, dim, keepdims=False), pairing))


def reduce_parts(halves):
    parts = [None] * PARTS
    for m, (v, w, _, _) in enumerate(ORDERS):
        got = across(halves[2 * m + 1], v)
        part = add(halves[2 * m], got).reshape(2, 2, 2, ROWS, COLS)
        parts[m] = halve(part, w - (v < w), w)
    for m, n in COUPLES:
        v, w = ORDERS[m][2:]
        couple = halve(halve(jnp.stack([parts[m], parts[n]]), 1, v), 1, w)
        parts[m], parts[n] = couple[0], couple[1]
    return parts


def reduce_z(parts):
    total = wide(parts[0])
    for m in range(1, PARTS):
        total = total + wide(z_swap(parts[m], m))
    total = total.astype(jnp.bfloat16)
    return (wide(total) + wide(z_swap(total, 7))).reshape(2, 32, COLS)


def double(array, dim, pairing):
    return jnp.stack([array, across(array, pairing)], axis=dim)


def gather_parts(pair):
    parts = [pair] + [z_swap(pair, m) for m in range(1, PARTS)]
    for m, n in COUPLES:
        v, w = ORDERS[m][2:]
        couple = double(double(jnp.stack([parts[m], parts[n]]), 1, w), 1, v)
        parts[m], parts[n] = couple[0], couple[1]
    halves = []
    for m, (v, w, _, _) in enumerate(ORDERS):
        keep = double(parts[m], w - (v < w), w).reshape(8, ROWS, COLS)
        halves += [keep, across(keep, v)]
    return halves


def local(activations, output_grads, master_weights, first_moment, second_moment, next_tokens):
    low = lax.axis_index("outer") % 8 < 4
    packed, packed_tokens, state = pack(
        activations, next_tokens, master_weights, first_moment, second_moment
    )
    got_acts = core_swap(packed)
    got_grads = core_swap(output_grads)
    got_state = z_swap(state, 7)
    got_tokens = core_swap(packed_tokens)
    halves = gradient_term(
        activations, got_acts, output_grads, got_grads, got_tokens, got_state
    )

    gradient = reduce_z(reduce_parts(halves))
    pairs = jnp.stack([jnp.where(low, state, got_state), jnp.where(low, got_state, state)], axis=1)
    updated = adamw_update(gradient, *pairs)
    new_master, new_first, new_second = (jnp.where(low, u[0], u[1]) for u in updated)
    pair = updated[0].astype(jnp.bfloat16).reshape(ROWS, COLS)

    kept_weights, mine, theirs = project(next_tokens, got_tokens, gather_parts(pair))
    projection = (mine + wide(core_swap(theirs))).astype(jnp.bfloat16)
    return (new_master, new_first, new_second, kept_weights, projection)


def solution(mesh):
    placed = (
        P(("outer", "inner"), None),
        P(("outer", "inner"), None),
        P(("inner", "outer"), None),
        P(("inner", "outer"), None),
        P(("inner", "outer"), None),
        P(("outer", "inner"), None),
    )
    return jax.shard_map(
        local,
        mesh=mesh,
        in_specs=placed,
        out_specs=(
            P(("inner", "outer"), None),
            P(("inner", "outer"), None),
            P(("inner", "outer"), None),
            P("inner", None),
            P(("outer", "inner"), None),
        ),
        check_vma=False,
    )
```

```python
import functools
import itertools

import jax
import jax.numpy as jnp
from jax import lax
from jax.experimental import pallas as pl
from jax.experimental.pallas import tpu as pltpu
from jax.sharding import PartitionSpec as P

ADAM_STEP = 10
beta_first = 0.9
beta_second = 0.95
learn_rate = 0.002
decay_rate = 0.1
adam_eps = 1e-08

AXES = ("outer", "inner")
SIZES = (2, 8, 4, 2, 2)
TOK = 256
COLS = 512
HALF = 4096
BLOCK = 256
BLOCKS = 16
PARTS = 2
ROWS = 128
PAIRS = 4

ORDERS = ((0, 2, 1, 3), (1, 3, 0, 2))


def moves(change):
    pairs = []
    for here in itertools.product(*(range(n) for n in SIZES)):
        source = target = 0
        for n, i, j in zip(SIZES, here, change(*here)):
            source, target = source * n + i, target * n + j
        pairs.append((source, target))
    return pairs


def paired(i, odd):
    if odd:
        return (i + 1) % 4 if i % 2 else (i - 1) % 4
    return i ^ 1


def pair(v, xh, z, y, xl, c):
    v = v ^ (2 * c)
    if v < 2:
        x = paired(xh * 2 + xl, v)
        return x // 2, z, y, x % 2, c
    return xh, z, paired(y, v - 2), xl, c


PAIRINGS = tuple(moves(functools.partial(pair, v)) for v in range(4))


def across(array, pairing):
    return lax.ppermute(array, AXES, PAIRINGS[pairing])


def z_swap(array, mask):
    return lax.ppermute(array, AXES, moves(lambda xh, z, y, xl, c: (xh, z ^ mask, y, xl, c)))


def core_swap(array):
    return lax.ppermute(array, AXES, moves(lambda xh, z, y, xl, c: (xh, z, y, xl, 1 - c)))


def place():
    outer, inner = lax.axis_index("outer"), lax.axis_index("inner")
    return outer // 8, outer % 8, inner // 4, (inner // 2) % 2, inner % 2


def columns_of(where, r, core):
    xh, _, y, xl, _ = where
    bits = [(r >> (3 - v)) & 1 for v in range(4)]
    a, b, c, d = (bits[v] + core * (bits[v ^ 2] - bits[v]) for v in range(4))
    to_xh, to_xl, to_y = xh ^ b, xl ^ (a ^ b), y ^ (2 * d + (c ^ d))
    block = ((to_y * 2 + to_xl) * 2 + core) * 2 + to_xh
    return pl.ds(pl.multiple_of(block * BLOCK, BLOCK), BLOCK)


def side_and_slot(m, r):
    bits = [(r >> (3 - v)) & 1 for v in range(4)]
    side = bits.pop(ORDERS[m][0])
    return side, bits[0] * 4 + bits[1] * 2 + bits[2]


def pair_starts(where, m):
    z = where[1]
    first = jnp.where(z < 4, z, 7 - z) ^ m
    return first * 32, (7 - first) * 32


ANY = pl.BlockSpec(memory_space=pl.ANY)
VMEM = pl.BlockSpec(memory_space=pltpu.VMEM)
PARAMS = pltpu.CompilerParams(vmem_limit_bytes=40 * 1024 * 1024)
WHOLE = pltpu.CompilerParams(vmem_limit_bytes=60 * 1024 * 1024)


def cost(flops, size):
    return pl.CostEstimate(flops=flops, bytes_accessed=size, transcendentals=0)


def run_all(copies):
    for copy in copies:
        copy.start()
    for copy in copies:
        copy.wait()


def theirs_of(source, packed, sems):
    where = place()
    return [
        pltpu.make_async_copy(
            source.at[:, columns_of(where, r, 1 - where[4])],
            packed.at[:, pl.ds(r * BLOCK, BLOCK)],
            sems.at[r],
        )
        for r in range(BLOCKS)
    ]


PACKED = jax.ShapeDtypeStruct((TOK, HALF), jnp.bfloat16)


DONE = jax.ShapeDtypeStruct((8, 128), jnp.float32)


def pack_acts_kernel(acts, packed, done, sems):
    done[...] = jnp.zeros_like(done)
    run_all(theirs_of(acts, packed, sems))


def pack_acts(acts):
    return pl.pallas_call(
        pack_acts_kernel,
        out_shape=(PACKED, DONE),
        in_specs=[ANY],
        out_specs=(ANY, VMEM),
        scratch_shapes=[pltpu.SemaphoreType.DMA((BLOCKS,))],
        compiler_params=WHOLE,
        cost_estimate=cost(0, 4 << 20),
        name="pack_acts",
    )(acts)


def pack_rest_kernel(tokens, master, first, second, _after, packed, state, done, sems):
    done[...] = jnp.zeros_like(done)
    run_all(
        theirs_of(tokens, packed, sems)
        + [
            pltpu.make_async_copy(source, state.at[i], sems.at[BLOCKS + i])
            for i, source in enumerate((master, first, second))
        ]
    )


def pack_rest(tokens, master, first, second, after):
    return pl.pallas_call(
        pack_rest_kernel,
        out_shape=(
            PACKED,
            jax.ShapeDtypeStruct((3, 32, COLS), jnp.float32),
            DONE,
        ),
        in_specs=[ANY] * 4 + [VMEM],
        out_specs=(ANY, ANY, VMEM),
        scratch_shapes=[pltpu.SemaphoreType.DMA((BLOCKS + 3,))],
        compiler_params=PARAMS,
        cost_estimate=cost(0, 5 << 20),
        name="pack_rest",
    )(tokens, master, first, second, after)


def term_kernel(acts, got, grads, got_grads, _after, *refs):
    halves = refs[: 2 * PARTS]
    both, grads_both, term, sems = refs[2 * PARTS :]
    where = place()
    own, other = [], []
    for r in range(BLOCKS):
        here = pl.ds(r * BLOCK, BLOCK)
        own.append(
            pltpu.make_async_copy(
                acts.at[:, columns_of(where, r, where[4])], both.at[:TOK, here], sems.at[r]
            )
        )
        other.append(
            pltpu.make_async_copy(got.at[:, here], both.at[TOK:, here], sems.at[BLOCKS + r])
        )
    for r in range(BLOCKS):
        own[r].start()
        other[r].start()
    grads_both[:TOK] = grads[...]
    grads_both[TOK:] = got_grads[...]
    starts = [pair_starts(where, m) for m in range(PAIRS)]
    for r in range(BLOCKS):
        own[r].wait()
        other[r].wait()
        term[r % 2] = lax.dot_general(
            both[:, r * BLOCK : (r + 1) * BLOCK],
            grads_both[...],
            (((0,), (0,)), ((), ())),
            preferred_element_type=jnp.float32,
        ).astype(jnp.bfloat16)
        for m in range(PAIRS):
            side, slot = side_and_slot(m // 2, r)
            for j in range(2):
                to = (m % 2) * 64 + j * 32
                halves[2 * (m // 2) + side][slot, to : to + 32] = term[
                    r % 2, pl.ds(pl.multiple_of(starts[m][j], 32), 32)
                ]


def gradient_term(acts, got, grads, got_grads, after):
    half = jax.ShapeDtypeStruct((8, ROWS, COLS), jnp.bfloat16)
    return pl.pallas_call(
        term_kernel,
        out_shape=(half,) * (2 * PARTS),
        in_specs=[ANY, ANY, VMEM, VMEM, VMEM],
        out_specs=(VMEM,) * (2 * PARTS),
        scratch_shapes=[
            pltpu.VMEM((2 * TOK, HALF), jnp.bfloat16),
            pltpu.VMEM((2 * TOK, COLS), jnp.bfloat16),
            pltpu.VMEM((2, BLOCK, COLS), jnp.bfloat16),
            pltpu.SemaphoreType.DMA((2 * BLOCKS,)),
        ],
        compiler_params=PARAMS,
        cost_estimate=cost(2 * 2 * TOK * HALF * COLS, 9 << 20),
        name="gradient_term",
    )(acts, got, grads, got_grads, after)


def add_kernel(dim, keep, got, *refs):
    next_keep, next_send = refs[-2:]
    blocks = keep.shape[0]
    inner = blocks >> (dim + 1)
    for slot in range(blocks):
        side = (slot // inner) % 2
        out = next_send if side else next_keep
        out[slot // (2 * inner) * inner + slot % inner] = (
            keep[slot].astype(jnp.float32) + got[slot].astype(jnp.float32)
        ).astype(jnp.bfloat16)


def add_halves(keep, got, dim, after=()):
    blocks = keep.shape[0]
    half = jax.ShapeDtypeStruct((blocks // 2, ROWS, COLS), jnp.bfloat16)
    return pl.pallas_call(
        functools.partial(add_kernel, dim),
        out_shape=(half, half),
        in_specs=[VMEM, VMEM] + [ANY] * len(after),
        out_specs=(VMEM, VMEM),
        compiler_params=PARAMS,
        cost_estimate=cost(blocks << 16, blocks * 3 << 17),
        name="add_halves",
    )(keep, got, *after)


def join_kernel(dim, here, got, both):
    blocks = here.shape[0]
    inner = blocks >> dim
    for slot in range(2 * blocks):
        source = got if (slot // inner) % 2 else here
        both[slot] = source[slot // (2 * inner) * inner + slot % inner]


def join(here, got, dim):
    blocks = here.shape[0]
    return pl.pallas_call(
        functools.partial(join_kernel, dim),
        out_shape=jax.ShapeDtypeStruct((2 * blocks, ROWS, COLS), jnp.bfloat16),
        in_specs=[VMEM, VMEM],
        out_specs=VMEM,
        compiler_params=PARAMS,
        cost_estimate=cost(0, blocks * 4 << 17),
        name="join",
    )(here, got)


STRIPE = 1024


def project_kernel(tokens, got, *refs):
    halves = refs[: 2 * PARTS]
    kept, mine, theirs, both, weights, total, sems = refs[2 * PARTS :]
    where = place()
    token_copies = [
        pltpu.make_async_copy(
            tokens.at[:, columns_of(where, r, where[4])],
            both.at[:TOK, pl.ds(r * BLOCK, BLOCK)],
            sems.at[r],
        )
        for r in range(BLOCKS)
    ]
    got_copies = [
        pltpu.make_async_copy(
            got.at[:, pl.ds(s * STRIPE, STRIPE)],
            both.at[TOK:, pl.ds(s * STRIPE, STRIPE)],
            sems.at[BLOCKS + s],
        )
        for s in range(HALF // STRIPE)
    ]
    per = STRIPE // BLOCK
    for s in range(HALF // STRIPE):
        for k in range(per):
            token_copies[s * per + k].start()
        got_copies[s].start()
    starts = [pair_starts(where, m) for m in range(PAIRS)]

    def keep_block(x_hi, block):
        kept[pl.ds(pl.multiple_of(x_hi * BLOCK, BLOCK), BLOCK)] = block

    for s in range(HALF // STRIPE):
        for k in range(per):
            for m in range(PAIRS):
                side, slot = side_and_slot(m // 2, s * per + k)
                for j in range(2):
                    at = pl.ds(pl.multiple_of(k * BLOCK + starts[m][j], 32), 32)
                    of = (m % 2) * 64 + j * 32
                    weights[s % 2, at] = halves[2 * (m // 2) + side][slot, of : of + 32]
            token_copies[s * per + k].wait()
        got_copies[s].wait()
        if s == 0:
            keep_block(where[0], weights[0, :BLOCK])

            @pl.when(where[4] == 1)
            def _():
                keep_block(1 - where[0], weights[0, 3 * BLOCK :])

        if s == 3:

            @pl.when(where[4] == 0)
            def _():
                keep_block(1 - where[0], weights[1, :BLOCK])

        product = jnp.dot(
            both[:, s * STRIPE : (s + 1) * STRIPE],
            weights[s % 2],
            preferred_element_type=jnp.float32,
        )
        if s == 0:
            total[...] = product
        elif s < HALF // STRIPE - 1:
            total[...] += product
        else:
            product += total[...]
            mine[...] = product[:TOK]
            theirs[...] = product[TOK:].astype(jnp.bfloat16)


def project(tokens, got, halves):
    return pl.pallas_call(
        project_kernel,
        out_shape=(
            jax.ShapeDtypeStruct((2 * BLOCK, COLS), jnp.bfloat16),
            jax.ShapeDtypeStruct((TOK, COLS), jnp.float32),
            jax.ShapeDtypeStruct((TOK, COLS), jnp.bfloat16),
        ),
        in_specs=[ANY, ANY] + [VMEM] * (2 * PARTS),
        out_specs=(VMEM,) * 3,
        scratch_shapes=[
            pltpu.VMEM((2 * TOK, HALF), jnp.bfloat16),
            pltpu.VMEM((2, STRIPE, COLS), jnp.bfloat16),
            pltpu.VMEM((2 * TOK, COLS), jnp.float32),
            pltpu.SemaphoreType.DMA((BLOCKS + HALF // STRIPE,)),
        ],
        compiler_params=PARAMS,
        cost_estimate=cost(2 * 2 * TOK * HALF * COLS, 9 << 20),
        name="project",
    )(tokens, got, *halves)


def adamw_update(gradient, master_weights, first_moment, second_moment):
    new_first = beta_first * first_moment + (1.0 - beta_first) * gradient
    new_second = beta_second * second_moment + (1.0 - beta_second) * gradient * gradient
    first_hat = new_first / (1.0 - beta_first**ADAM_STEP)
    second_hat = new_second / (1.0 - beta_second**ADAM_STEP)
    new_master = master_weights - learn_rate * (
        first_hat / (jnp.sqrt(second_hat) + adam_eps) + decay_rate * master_weights
    )
    return (new_master, new_first, new_second)


def wide(array):
    return array.astype(jnp.float32)


def add(keep, got):
    return (wide(keep) + wide(got)).astype(jnp.bfloat16)


def halve(array, dim, pairing):
    keep = lax.index_in_dim(array, 0, dim, keepdims=False)
    return add(keep, across(lax.index_in_dim(array, 1, dim, keepdims=False), pairing))


def reduce_parts(halves, tokens, state):
    parts = []
    for i, (v, w, p, q) in enumerate(ORDERS):
        keep, got = halves[2 * i], across(halves[2 * i + 1], v)
        keep, send = add_halves(keep, got, w - (v < w), (tokens,) if i else ())
        got = across(send, w)
        keep, send = add_halves(keep, got, sorted((p, q)).index(p), (state,) if i else ())
        got = across(send, p)
        keep, send = add_halves(keep, got, 0)
        parts.append((wide(keep) + wide(across(send, q))).astype(jnp.bfloat16).reshape(ROWS, COLS))
    return parts


def reduce_z(parts):
    total = wide(parts[0][:64])
    for m in range(1, PAIRS):
        rows = parts[m // 2][(m % 2) * 64 : (m % 2) * 64 + 64]
        total = total + wide(z_swap(rows, m))
    total = total.astype(jnp.bfloat16)
    return (wide(total) + wide(z_swap(total, 7))).reshape(2, 32, COLS)


def gather_parts(pair):
    pairs = [pair] + [z_swap(pair, m) for m in range(1, PAIRS)]
    halves = []
    for i, (v, w, p, q) in enumerate(ORDERS):
        part = jnp.concatenate(pairs[2 * i : 2 * i + 2], axis=0)[None]
        for bit, dim in ((q, 0), (p, sorted((p, q)).index(p)), (w, w - (v < w))):
            part = join(part, across(part, bit), dim)
        halves += [part, across(part, v)]
    return halves


def local(activations, output_grads, master_weights, first_moment, second_moment, next_tokens):
    low = lax.axis_index("outer") % 8 < 4
    packed, packed_acts = pack_acts(activations)
    packed_tokens, state, packed_all = pack_rest(
        next_tokens, master_weights, first_moment, second_moment, packed_acts
    )
    got_acts, got_grads = core_swap(packed), core_swap(output_grads)
    halves = gradient_term(
        activations, got_acts, output_grads, got_grads, packed_all
    )
    got_state = z_swap(state, 7)
    got_tokens = core_swap(packed_tokens)

    gradient = reduce_z(reduce_parts(halves, got_tokens, got_state))
    pairs = jnp.stack([jnp.where(low, state, got_state), jnp.where(low, got_state, state)], axis=1)
    updated = adamw_update(gradient, *pairs)
    new_master, new_first, new_second = (jnp.where(low, u[0], u[1]) for u in updated)
    rows = updated[0].astype(jnp.bfloat16).reshape(64, COLS)

    kept_weights, mine, theirs = project(next_tokens, got_tokens, gather_parts(rows))
    projection = (mine + wide(core_swap(theirs))).astype(jnp.bfloat16)
    return (new_master, new_first, new_second, kept_weights, projection)


def solution(mesh):
    placed = (
        P(("outer", "inner"), None),
        P(("outer", "inner"), None),
        P(("inner", "outer"), None),
        P(("inner", "outer"), None),
        P(("inner", "outer"), None),
        P(("outer", "inner"), None),
    )
    return jax.shard_map(
        local,
        mesh=mesh,
        in_specs=placed,
        out_specs=(
            P(("inner", "outer"), None),
            P(("inner", "outer"), None),
            P(("inner", "outer"), None),
            P("inner", None),
            P(("outer", "inner"), None),
        ),
        check_vma=False,
    )
```

```python
import functools
import itertools

import jax
import jax.numpy as jnp
from jax import lax
from jax.experimental import pallas as pl
from jax.experimental.pallas import tpu as pltpu
from jax.sharding import PartitionSpec as P

ADAM_STEP = 10
beta_first = 0.9
beta_second = 0.95
learn_rate = 0.002
decay_rate = 0.1
adam_eps = 1e-08

AXES = ("outer", "inner")
SIZES = (2, 8, 4, 2, 2)
TOK = 256
COLS = 512
HALF = 4096
BLOCK = 256
BLOCKS = 16
PARTS = 4
ROWS = 64

ORDERS = ((0, 2, 1, 3), (1, 3, 0, 2), (2, 0, 3, 1), (3, 1, 2, 0))


def moves(change):
    pairs = []
    for here in itertools.product(*(range(n) for n in SIZES)):
        source = target = 0
        for n, i, j in zip(SIZES, here, change(*here)):
            source, target = source * n + i, target * n + j
        pairs.append((source, target))
    return pairs


def paired(i, odd):
    if odd:
        return (i + 1) % 4 if i % 2 else (i - 1) % 4
    return i ^ 1


def pair(v, xh, z, y, xl, c):
    v = v ^ (2 * c)
    if v < 2:
        x = paired(xh * 2 + xl, v)
        return x // 2, z, y, x % 2, c
    return xh, z, paired(y, v - 2), xl, c


PAIRINGS = tuple(moves(functools.partial(pair, v)) for v in range(4))


def across(array, pairing):
    return lax.ppermute(array, AXES, PAIRINGS[pairing])


def z_swap(array, mask):
    return lax.ppermute(array, AXES, moves(lambda xh, z, y, xl, c: (xh, z ^ mask, y, xl, c)))


def core_swap(array):
    return lax.ppermute(array, AXES, moves(lambda xh, z, y, xl, c: (xh, z, y, xl, 1 - c)))


def place():
    outer, inner = lax.axis_index("outer"), lax.axis_index("inner")
    return outer // 8, outer % 8, inner // 4, (inner // 2) % 2, inner % 2


def columns_of(where, r, core):
    xh, _, y, xl, _ = where
    bits = [(r >> (3 - v)) & 1 for v in range(4)]
    a, b, c, d = (bits[v] + core * (bits[v ^ 2] - bits[v]) for v in range(4))
    to_xh, to_xl, to_y = xh ^ b, xl ^ (a ^ b), y ^ (2 * d + (c ^ d))
    block = ((to_y * 2 + to_xl) * 2 + core) * 2 + to_xh
    return pl.ds(pl.multiple_of(block * BLOCK, BLOCK), BLOCK)


def side_and_slot(m, r):
    bits = [(r >> (3 - v)) & 1 for v in range(4)]
    side = bits.pop(ORDERS[m][0])
    return side, bits[0] * 4 + bits[1] * 2 + bits[2]


def pair_starts(where, m):
    z = where[1]
    first = jnp.where(z < 4, z, 7 - z) ^ m
    return first * 32, (7 - first) * 32


ANY = pl.BlockSpec(memory_space=pl.ANY)
VMEM = pl.BlockSpec(memory_space=pltpu.VMEM)
PARAMS = pltpu.CompilerParams(vmem_limit_bytes=40 * 1024 * 1024)
WHOLE = pltpu.CompilerParams(vmem_limit_bytes=60 * 1024 * 1024)


def cost(flops, size):
    return pl.CostEstimate(flops=flops, bytes_accessed=size, transcendentals=0)


def run_all(copies):
    for copy in copies:
        copy.start()
    for copy in copies:
        copy.wait()


def theirs_of(source, packed, sems):
    where = place()
    return [
        pltpu.make_async_copy(
            source.at[:, columns_of(where, r, 1 - where[4])],
            packed.at[:, pl.ds(r * BLOCK, BLOCK)],
            sems.at[r],
        )
        for r in range(BLOCKS)
    ]


PACKED = jax.ShapeDtypeStruct((TOK, HALF), jnp.bfloat16)


DONE = jax.ShapeDtypeStruct((8, 128), jnp.float32)


def pack_acts_kernel(acts, grads, packed, done, sems):
    done[...] = jnp.zeros_like(done)
    run_all(
        theirs_of(acts, packed, sems)
        + [pltpu.make_async_copy(grads, packed.at[:, pl.ds(HALF, COLS)], sems.at[BLOCKS])]
    )


def pack_acts(acts, grads):
    return pl.pallas_call(
        pack_acts_kernel,
        out_shape=(jax.ShapeDtypeStruct((TOK, HALF + COLS), jnp.bfloat16), DONE),
        in_specs=[ANY, ANY],
        out_specs=(VMEM, VMEM),
        scratch_shapes=[pltpu.SemaphoreType.DMA((BLOCKS + 1,))],
        compiler_params=WHOLE,
        cost_estimate=cost(0, 4 << 20),
        name="pack_acts",
    )(acts, grads)


def pack_rest_kernel(tokens, master, first, second, _after, packed, state, done, sems):
    done[...] = jnp.zeros_like(done)
    run_all(
        theirs_of(tokens, packed, sems)
        + [
            pltpu.make_async_copy(source, state.at[i], sems.at[BLOCKS + i])
            for i, source in enumerate((master, first, second))
        ]
    )


def pack_rest(tokens, master, first, second, after):
    return pl.pallas_call(
        pack_rest_kernel,
        out_shape=(
            PACKED,
            jax.ShapeDtypeStruct((3, 32, COLS), jnp.float32),
            DONE,
        ),
        in_specs=[ANY] * 4 + [VMEM],
        out_specs=(VMEM, VMEM, VMEM),
        scratch_shapes=[pltpu.SemaphoreType.DMA((BLOCKS + 3,))],
        compiler_params=PARAMS,
        cost_estimate=cost(0, 5 << 20),
        name="pack_rest",
    )(tokens, master, first, second, after)


def term_kernel(acts, got, grads, _after, *refs):
    halves = refs[: 2 * PARTS]
    both, grads_both, term, sems = refs[2 * PARTS :]
    where = place()
    own, other = [], []
    for r in range(BLOCKS):
        here = pl.ds(r * BLOCK, BLOCK)
        own.append(
            pltpu.make_async_copy(
                acts.at[:, columns_of(where, r, where[4])], both.at[:TOK, here], sems.at[r]
            )
        )
        other.append(
            pltpu.make_async_copy(got.at[:, here], both.at[TOK:, here], sems.at[BLOCKS + r])
        )
    for r in range(BLOCKS):
        own[r].start()
        other[r].start()
    got_grads = pltpu.make_async_copy(
        got.at[:, pl.ds(HALF, COLS)], grads_both.at[TOK:], sems.at[2 * BLOCKS]
    )
    got_grads.start()
    grads_both[:TOK] = grads[...]
    got_grads.wait()
    starts = [pair_starts(where, m) for m in range(PARTS)]
    for r in range(BLOCKS):
        own[r].wait()
        other[r].wait()
        term[r % 2] = lax.dot_general(
            both[:, r * BLOCK : (r + 1) * BLOCK],
            grads_both[...],
            (((0,), (0,)), ((), ())),
            preferred_element_type=jnp.float32,
        ).astype(jnp.bfloat16)
        for m in range(PARTS):
            side, slot = side_and_slot(m, r)
            for j in range(2):
                halves[2 * m + side][slot, j * 32 : j * 32 + 32] = term[
                    r % 2, pl.ds(pl.multiple_of(starts[m][j], 32), 32)
                ]


def gradient_term(acts, got, grads, after):
    half = jax.ShapeDtypeStruct((8, ROWS, COLS), jnp.bfloat16)
    return pl.pallas_call(
        term_kernel,
        out_shape=(half,) * (2 * PARTS),
        in_specs=[ANY, ANY, VMEM, VMEM],
        out_specs=(VMEM,) * (2 * PARTS),
        scratch_shapes=[
            pltpu.VMEM((2 * TOK, HALF), jnp.bfloat16),
            pltpu.VMEM((2 * TOK, COLS), jnp.bfloat16),
            pltpu.VMEM((2, BLOCK, COLS), jnp.bfloat16),
            pltpu.SemaphoreType.DMA((2 * BLOCKS + 1,)),
        ],
        compiler_params=PARAMS,
        cost_estimate=cost(2 * 2 * TOK * HALF * COLS, 9 << 20),
        name="gradient_term",
    )(acts, got, grads, after)


def add_kernel(dim, keep, got, *refs):
    next_keep, next_send = refs[-2:]
    blocks = keep.shape[0]
    inner = blocks >> (dim + 1)
    for slot in range(blocks):
        side = (slot // inner) % 2
        out = next_send if side else next_keep
        out[slot // (2 * inner) * inner + slot % inner] = (
            keep[slot].astype(jnp.float32) + got[slot].astype(jnp.float32)
        ).astype(jnp.bfloat16)


def add_halves(keep, got, dim, after=()):
    blocks = keep.shape[0]
    half = jax.ShapeDtypeStruct((blocks // 2, ROWS, COLS), jnp.bfloat16)
    return pl.pallas_call(
        functools.partial(add_kernel, dim),
        out_shape=(half, half),
        in_specs=[VMEM, VMEM] + [ANY] * len(after),
        out_specs=(VMEM, VMEM),
        compiler_params=PARAMS,
        cost_estimate=cost(blocks << 16, blocks * 3 << 17),
        name="add_halves",
    )(keep, got, *after)


def join_kernel(dim, here, got, both):
    blocks = here.shape[0]
    inner = blocks >> dim
    for slot in range(2 * blocks):
        source = got if (slot // inner) % 2 else here
        both[slot] = source[slot // (2 * inner) * inner + slot % inner]


def join(here, got, dim):
    blocks = here.shape[0]
    return pl.pallas_call(
        functools.partial(join_kernel, dim),
        out_shape=jax.ShapeDtypeStruct((2 * blocks, ROWS, COLS), jnp.bfloat16),
        in_specs=[VMEM, VMEM],
        out_specs=VMEM,
        compiler_params=PARAMS,
        cost_estimate=cost(0, blocks * 4 << 17),
        name="join",
    )(here, got)


STRIPE = 1024


def project_kernel(tokens, got, *refs):
    halves = refs[: 2 * PARTS]
    kept, mine, theirs, both, weights, total, sems = refs[2 * PARTS :]
    where = place()
    token_copies = [
        pltpu.make_async_copy(
            tokens.at[:, columns_of(where, r, where[4])],
            both.at[:TOK, pl.ds(r * BLOCK, BLOCK)],
            sems.at[r],
        )
        for r in range(BLOCKS)
    ]
    got_copies = [
        pltpu.make_async_copy(
            got.at[:, pl.ds(s * STRIPE, STRIPE)],
            both.at[TOK:, pl.ds(s * STRIPE, STRIPE)],
            sems.at[BLOCKS + s],
        )
        for s in range(HALF // STRIPE)
    ]
    per = STRIPE // BLOCK
    for s in range(HALF // STRIPE):
        for k in range(per):
            token_copies[s * per + k].start()
        got_copies[s].start()
    starts = [pair_starts(where, m) for m in range(PARTS)]

    def keep_block(x_hi, block):
        kept[pl.ds(pl.multiple_of(x_hi * BLOCK, BLOCK), BLOCK)] = block

    for s in range(HALF // STRIPE):
        for k in range(per):
            for m in range(PARTS):
                side, slot = side_and_slot(m, s * per + k)
                for j in range(2):
                    at = pl.ds(pl.multiple_of(k * BLOCK + starts[m][j], 32), 32)
                    weights[s % 2, at] = halves[2 * m + side][slot, j * 32 : j * 32 + 32]
            token_copies[s * per + k].wait()
        got_copies[s].wait()
        if s == 0:
            keep_block(where[0], weights[0, :BLOCK])

            @pl.when(where[4] == 1)
            def _():
                keep_block(1 - where[0], weights[0, 3 * BLOCK :])

        if s == 3:

            @pl.when(where[4] == 0)
            def _():
                keep_block(1 - where[0], weights[1, :BLOCK])

        product = jnp.dot(
            both[:, s * STRIPE : (s + 1) * STRIPE],
            weights[s % 2],
            preferred_element_type=jnp.float32,
        )
        if s == 0:
            total[...] = product
        elif s < HALF // STRIPE - 1:
            total[...] += product
        else:
            product += total[...]
            mine[...] = product[:TOK]
            theirs[...] = product[TOK:].astype(jnp.bfloat16)


def project(tokens, got, halves):
    return pl.pallas_call(
        project_kernel,
        out_shape=(
            jax.ShapeDtypeStruct((2 * BLOCK, COLS), jnp.bfloat16),
            jax.ShapeDtypeStruct((TOK, COLS), jnp.float32),
            jax.ShapeDtypeStruct((TOK, COLS), jnp.bfloat16),
        ),
        in_specs=[ANY, ANY] + [VMEM] * (2 * PARTS),
        out_specs=(VMEM,) * 3,
        scratch_shapes=[
            pltpu.VMEM((2 * TOK, HALF), jnp.bfloat16),
            pltpu.VMEM((2, STRIPE, COLS), jnp.bfloat16),
            pltpu.VMEM((2 * TOK, COLS), jnp.float32),
            pltpu.SemaphoreType.DMA((BLOCKS + HALF // STRIPE,)),
        ],
        compiler_params=PARAMS,
        cost_estimate=cost(2 * 2 * TOK * HALF * COLS, 9 << 20),
        name="project",
    )(tokens, got, *halves)


def adamw_update(gradient, master_weights, first_moment, second_moment):
    new_first = beta_first * first_moment + (1.0 - beta_first) * gradient
    new_second = beta_second * second_moment + (1.0 - beta_second) * gradient * gradient
    first_hat = new_first / (1.0 - beta_first**ADAM_STEP)
    second_hat = new_second / (1.0 - beta_second**ADAM_STEP)
    new_master = master_weights - learn_rate * (
        first_hat / (jnp.sqrt(second_hat) + adam_eps) + decay_rate * master_weights
    )
    return (new_master, new_first, new_second)


def wide(array):
    return array.astype(jnp.float32)


def add(keep, got):
    return (wide(keep) + wide(got)).astype(jnp.bfloat16)


def halve(array, dim, pairing):
    keep = lax.index_in_dim(array, 0, dim, keepdims=False)
    return add(keep, across(lax.index_in_dim(array, 1, dim, keepdims=False), pairing))


def reduce_parts(halves, after):
    parts = []
    for m, (v, w, p, q) in enumerate(ORDERS):
        keep, got = halves[2 * m], across(halves[2 * m + 1], v)
        keep, send = add_halves(keep, got, w - (v < w), () if m else after)
        keep, send = add_halves(keep, across(send, w), sorted((p, q)).index(p))
        keep, send = add_halves(keep, across(send, p), 0)
        total = wide(keep[0]) + wide(across(send[0], q))
        parts.append(total.astype(jnp.bfloat16) if m else total)
    return parts


def reduce_z(parts):
    total = parts[0]
    for m in range(1, PARTS):
        total = total + wide(z_swap(parts[m], m))
    total = total.astype(jnp.bfloat16)
    return (wide(total) + wide(z_swap(total, 7))).reshape(2, 32, COLS)


def gather_parts(rows):
    halves = []
    for m, (v, w, p, q) in enumerate(ORDERS):
        part = (z_swap(rows, m) if m else rows)[None]
        for bit, dim in ((q, 0), (p, sorted((p, q)).index(p)), (w, w - (v < w))):
            part = join(part, across(part, bit), dim)
        halves += [part, across(part, v)]
    return halves


def local(activations, output_grads, master_weights, first_moment, second_moment, next_tokens):
    low = lax.axis_index("outer") % 8 < 4
    packed, packed_acts = pack_acts(activations, output_grads)
    packed_tokens, state, packed_all = pack_rest(
        next_tokens, master_weights, first_moment, second_moment, packed_acts
    )
    halves = gradient_term(activations, core_swap(packed), output_grads, packed_all)
    got_state = z_swap(state, 7)
    got_tokens = core_swap(packed_tokens)

    gradient = reduce_z(reduce_parts(halves, (got_tokens, got_state)))
    pairs = jnp.stack([jnp.where(low, state, got_state), jnp.where(low, got_state, state)], axis=1)
    updated = adamw_update(gradient, *pairs)
    new_master, new_first, new_second = (jnp.where(low, u[0], u[1]) for u in updated)
    rows = updated[0].astype(jnp.bfloat16).reshape(64, COLS)

    kept_weights, mine, theirs = project(next_tokens, got_tokens, gather_parts(rows))
    projection = (mine + wide(core_swap(theirs))).astype(jnp.bfloat16)
    return (new_master, new_first, new_second, kept_weights, projection)


def solution(mesh):
    placed = (
        P(("outer", "inner"), None),
        P(("outer", "inner"), None),
        P(("inner", "outer"), None),
        P(("inner", "outer"), None),
        P(("inner", "outer"), None),
        P(("outer", "inner"), None),
    )
    return jax.shard_map(
        local,
        mesh=mesh,
        in_specs=placed,
        out_specs=(
            P(("inner", "outer"), None),
            P(("inner", "outer"), None),
            P(("inner", "outer"), None),
            P("inner", None),
            P(("outer", "inner"), None),
        ),
        check_vma=False,
    )
```

```python
import functools
import itertools

import jax
import jax.numpy as jnp
from jax import lax
from jax.experimental import pallas as pl
from jax.experimental.pallas import tpu as pltpu
from jax.sharding import PartitionSpec as P

ADAM_STEP = 10
beta_first = 0.9
beta_second = 0.95
learn_rate = 0.002
decay_rate = 0.1
adam_eps = 1e-08

AXES = ("outer", "inner")
SIZES = (2, 8, 4, 2, 2)
TOK = 256
COLS = 512
HALF = 4096
BLOCK = 256
BLOCKS = 16
PARTS = 4
ROWS = 64

ORDERS = ((0, 2, 1, 3), (1, 3, 0, 2), (2, 0, 3, 1), (3, 1, 2, 0))


def moves(change):
    pairs = []
    for here in itertools.product(*(range(n) for n in SIZES)):
        source = target = 0
        for n, i, j in zip(SIZES, here, change(*here)):
            source, target = source * n + i, target * n + j
        pairs.append((source, target))
    return pairs


def paired(i, odd):
    if odd:
        return (i + 1) % 4 if i % 2 else (i - 1) % 4
    return i ^ 1


def pair(v, xh, z, y, xl, c):
    v = v ^ (2 * c)
    if v < 2:
        x = paired(xh * 2 + xl, v)
        return x // 2, z, y, x % 2, c
    return xh, z, paired(y, v - 2), xl, c


PAIRINGS = tuple(moves(functools.partial(pair, v)) for v in range(4))


def across(array, pairing):
    return lax.ppermute(array, AXES, PAIRINGS[pairing])


def z_swap(array, mask):
    return lax.ppermute(array, AXES, moves(lambda xh, z, y, xl, c: (xh, z ^ mask, y, xl, c)))


def core_swap(array):
    return lax.ppermute(array, AXES, moves(lambda xh, z, y, xl, c: (xh, z, y, xl, 1 - c)))


def place():
    outer, inner = lax.axis_index("outer"), lax.axis_index("inner")
    return outer // 8, outer % 8, inner // 4, (inner // 2) % 2, inner % 2


def columns_of(where, r, core):
    xh, _, y, xl, _ = where
    bits = [(r >> (3 - v)) & 1 for v in range(4)]
    a, b, c, d = (bits[v] + core * (bits[v ^ 2] - bits[v]) for v in range(4))
    to_xh, to_xl, to_y = xh ^ b, xl ^ (a ^ b), y ^ (2 * d + (c ^ d))
    block = ((to_y * 2 + to_xl) * 2 + core) * 2 + to_xh
    return pl.ds(pl.multiple_of(block * BLOCK, BLOCK), BLOCK)


def side_and_slot(m, r):
    bits = [(r >> (3 - v)) & 1 for v in range(4)]
    side = bits.pop(ORDERS[m][0])
    return side, bits[0] * 4 + bits[1] * 2 + bits[2]


def pair_starts(where, m):
    z = where[1]
    first = jnp.where(z < 4, z, 7 - z) ^ m
    return first * 32, (7 - first) * 32


ANY = pl.BlockSpec(memory_space=pl.ANY)
VMEM = pl.BlockSpec(memory_space=pltpu.VMEM)
PARAMS = pltpu.CompilerParams(vmem_limit_bytes=40 * 1024 * 1024)
WHOLE = pltpu.CompilerParams(vmem_limit_bytes=60 * 1024 * 1024)


def cost(flops, size):
    return pl.CostEstimate(flops=flops, bytes_accessed=size, transcendentals=0)


def run_all(copies):
    for copy in copies:
        copy.start()
    for copy in copies:
        copy.wait()


def theirs_of(source, packed, sems, pieces=1):
    where = place()
    rows = TOK // pieces
    return [
        pltpu.make_async_copy(
            source.at[pl.ds(i * rows, rows), columns_of(where, r, 1 - where[4])],
            packed.at[pl.ds(i * rows, rows), pl.ds(r * BLOCK, BLOCK)],
            sems.at[r * pieces + i],
        )
        for r in range(BLOCKS)
        for i in range(pieces)
    ]


PACKED = jax.ShapeDtypeStruct((TOK, HALF), jnp.bfloat16)


DONE = jax.ShapeDtypeStruct((8, 128), jnp.float32)


PIECES = 4


def pack_acts_kernel(acts, grads, packed, done, sems):
    done[...] = jnp.zeros_like(done)
    run_all(
        theirs_of(acts, packed, sems, PIECES)
        + [pltpu.make_async_copy(grads, packed.at[:, pl.ds(HALF, COLS)], sems.at[BLOCKS * PIECES])]
    )


def pack_acts(acts, grads):
    return pl.pallas_call(
        pack_acts_kernel,
        out_shape=(jax.ShapeDtypeStruct((TOK, HALF + COLS), jnp.bfloat16), DONE),
        in_specs=[ANY, ANY],
        out_specs=(VMEM, VMEM),
        scratch_shapes=[pltpu.SemaphoreType.DMA((BLOCKS * PIECES + 1,))],
        compiler_params=WHOLE,
        cost_estimate=cost(0, 4 << 20),
        name="pack_acts",
    )(acts, grads)


def pack_rest_kernel(tokens, master, first, second, _after, packed, state, done, sems):
    done[...] = jnp.zeros_like(done)
    run_all(
        theirs_of(tokens, packed, sems)
        + [
            pltpu.make_async_copy(source, state.at[i], sems.at[BLOCKS + i])
            for i, source in enumerate((master, first, second))
        ]
    )


def pack_rest(tokens, master, first, second, after):
    return pl.pallas_call(
        pack_rest_kernel,
        out_shape=(
            PACKED,
            jax.ShapeDtypeStruct((3, 32, COLS), jnp.float32),
            DONE,
        ),
        in_specs=[ANY] * 4 + [VMEM],
        out_specs=(VMEM, VMEM, VMEM),
        scratch_shapes=[pltpu.SemaphoreType.DMA((BLOCKS + 3,))],
        compiler_params=PARAMS,
        cost_estimate=cost(0, 5 << 20),
        name="pack_rest",
    )(tokens, master, first, second, after)


def term_kernel(acts, got, grads, _after, *refs):
    halves = refs[: 2 * PARTS]
    both, grads_both, term, sems = refs[2 * PARTS :]
    where = place()
    own, other = [], []
    for r in range(BLOCKS):
        here = pl.ds(r * BLOCK, BLOCK)
        own.append(
            pltpu.make_async_copy(
                acts.at[:, columns_of(where, r, where[4])], both.at[:TOK, here], sems.at[r]
            )
        )
        other.append(
            pltpu.make_async_copy(got.at[:, here], both.at[TOK:, here], sems.at[BLOCKS + r])
        )
    for r in range(BLOCKS):
        own[r].start()
        other[r].start()
    got_grads = pltpu.make_async_copy(
        got.at[:, pl.ds(HALF, COLS)], grads_both.at[TOK:], sems.at[2 * BLOCKS]
    )
    got_grads.start()
    grads_both[:TOK] = grads[...]
    got_grads.wait()
    starts = [pair_starts(where, m) for m in range(PARTS)]
    for r in range(BLOCKS):
        own[r].wait()
        other[r].wait()
        term[r % 2] = lax.dot_general(
            both[:, r * BLOCK : (r + 1) * BLOCK],
            grads_both[...],
            (((0,), (0,)), ((), ())),
            preferred_element_type=jnp.float32,
        ).astype(jnp.bfloat16)
        for m in range(PARTS):
            side, slot = side_and_slot(m, r)
            for j in range(2):
                halves[2 * m + side][slot, j * 32 : j * 32 + 32] = term[
                    r % 2, pl.ds(pl.multiple_of(starts[m][j], 32), 32)
                ]


def gradient_term(acts, got, grads, after):
    half = jax.ShapeDtypeStruct((8, ROWS, COLS), jnp.bfloat16)
    return pl.pallas_call(
        term_kernel,
        out_shape=(half,) * (2 * PARTS),
        in_specs=[ANY, ANY, VMEM, VMEM],
        out_specs=(VMEM,) * (2 * PARTS),
        scratch_shapes=[
            pltpu.VMEM((2 * TOK, HALF), jnp.bfloat16),
            pltpu.VMEM((2 * TOK, COLS), jnp.bfloat16),
            pltpu.VMEM((2, BLOCK, COLS), jnp.bfloat16),
            pltpu.SemaphoreType.DMA((2 * BLOCKS + 1,)),
        ],
        compiler_params=PARAMS,
        cost_estimate=cost(2 * 2 * TOK * HALF * COLS, 9 << 20),
        name="gradient_term",
    )(acts, got, grads, after)


def add_kernel(dims, n_outs, *refs):
    outs = refs[-n_outs:]
    for i, dim in enumerate(dims):
        keep, got = refs[2 * i : 2 * i + 2]
        blocks = keep.shape[0]
        inner = blocks >> (dim + 1)
        for slot in range(blocks):
            outs[2 * i + (slot // inner) % 2][slot // (2 * inner) * inner + slot % inner] = (
                keep[slot].astype(jnp.float32) + got[slot].astype(jnp.float32)
            ).astype(jnp.bfloat16)


def add_halves(pairs, dims, after=(), through=()):
    blocks = pairs[0].shape[0]
    half = jax.ShapeDtypeStruct((blocks // 2, ROWS, COLS), jnp.bfloat16)
    n, first = len(pairs), len(pairs) + len(after)
    return pl.pallas_call(
        functools.partial(add_kernel, dims, n + len(through)),
        out_shape=(half,) * n + tuple(jax.ShapeDtypeStruct(t.shape, t.dtype) for t in through),
        in_specs=[VMEM] * n + [ANY] * (len(after) + len(through)),
        out_specs=(VMEM,) * n + (ANY,) * len(through),
        input_output_aliases={first + i: n + i for i in range(len(through))},
        compiler_params=PARAMS,
        cost_estimate=cost(n * blocks << 15, n * blocks * 3 << 16),
        name="add_halves",
    )(*pairs, *after, *through)


def join_kernel(dim, here, got, both):
    blocks = here.shape[0]
    inner = blocks >> dim
    for slot in range(2 * blocks):
        source = got if (slot // inner) % 2 else here
        both[slot] = source[slot // (2 * inner) * inner + slot % inner]


def join(here, got, dim):
    blocks = here.shape[0]
    return pl.pallas_call(
        functools.partial(join_kernel, dim),
        out_shape=jax.ShapeDtypeStruct((2 * blocks, ROWS, COLS), jnp.bfloat16),
        in_specs=[VMEM, VMEM],
        out_specs=VMEM,
        compiler_params=PARAMS,
        cost_estimate=cost(0, blocks * 4 << 17),
        name="join",
    )(here, got)


STRIPE = 1024


def project_kernel(tokens, got, *refs):
    halves = refs[: 2 * PARTS]
    kept, mine, theirs, both, weights, total, sems = refs[2 * PARTS :]
    where = place()
    token_copies = [
        pltpu.make_async_copy(
            tokens.at[:, columns_of(where, r, where[4])],
            both.at[:TOK, pl.ds(r * BLOCK, BLOCK)],
            sems.at[r],
        )
        for r in range(BLOCKS)
    ]
    got_copies = [
        pltpu.make_async_copy(
            got.at[:, pl.ds(s * STRIPE, STRIPE)],
            both.at[TOK:, pl.ds(s * STRIPE, STRIPE)],
            sems.at[BLOCKS + s],
        )
        for s in range(HALF // STRIPE)
    ]
    per = STRIPE // BLOCK
    for s in range(HALF // STRIPE):
        for k in range(per):
            token_copies[s * per + k].start()
        got_copies[s].start()
    starts = [pair_starts(where, m) for m in range(PARTS)]

    def keep_block(x_hi, block):
        kept[pl.ds(pl.multiple_of(x_hi * BLOCK, BLOCK), BLOCK)] = block

    for s in range(HALF // STRIPE):
        for k in range(per):
            for m in range(PARTS):
                side, slot = side_and_slot(m, s * per + k)
                for j in range(2):
                    at = pl.ds(pl.multiple_of(k * BLOCK + starts[m][j], 32), 32)
                    weights[s % 2, at] = halves[2 * m + side][slot, j * 32 : j * 32 + 32]
            token_copies[s * per + k].wait()
        got_copies[s].wait()
        if s == 0:
            keep_block(where[0], weights[0, :BLOCK])

            @pl.when(where[4] == 1)
            def _():
                keep_block(1 - where[0], weights[0, 3 * BLOCK :])

        if s == 3:

            @pl.when(where[4] == 0)
            def _():
                keep_block(1 - where[0], weights[1, :BLOCK])

        product = jnp.dot(
            both[:, s * STRIPE : (s + 1) * STRIPE],
            weights[s % 2],
            preferred_element_type=jnp.float32,
        )
        if s == 0:
            total[...] = product
        elif s < HALF // STRIPE - 1:
            total[...] += product
        else:
            product += total[...]
            mine[...] = product[:TOK]
            theirs[...] = product[TOK:].astype(jnp.bfloat16)


def project(tokens, got, halves):
    return pl.pallas_call(
        project_kernel,
        out_shape=(
            jax.ShapeDtypeStruct((2 * BLOCK, COLS), jnp.bfloat16),
            jax.ShapeDtypeStruct((TOK, COLS), jnp.float32),
            jax.ShapeDtypeStruct((TOK, COLS), jnp.bfloat16),
        ),
        in_specs=[ANY, ANY] + [VMEM] * (2 * PARTS),
        out_specs=(VMEM,) * 3,
        scratch_shapes=[
            pltpu.VMEM((2 * TOK, HALF), jnp.bfloat16),
            pltpu.VMEM((2, STRIPE, COLS), jnp.bfloat16),
            pltpu.VMEM((2 * TOK, COLS), jnp.float32),
            pltpu.SemaphoreType.DMA((BLOCKS + HALF // STRIPE,)),
        ],
        compiler_params=PARAMS,
        cost_estimate=cost(2 * 2 * TOK * HALF * COLS, 9 << 20),
        name="project",
    )(tokens, got, *halves)


def adamw_update(gradient, master_weights, first_moment, second_moment):
    new_first = beta_first * first_moment + (1.0 - beta_first) * gradient
    new_second = beta_second * second_moment + (1.0 - beta_second) * gradient * gradient
    first_hat = new_first / (1.0 - beta_first**ADAM_STEP)
    second_hat = new_second / (1.0 - beta_second**ADAM_STEP)
    new_master = master_weights - learn_rate * (
        first_hat / (jnp.sqrt(second_hat) + adam_eps) + decay_rate * master_weights
    )
    return (new_master, new_first, new_second)


def wide(array):
    return array.astype(jnp.float32)


def add(keep, got):
    return (wide(keep) + wide(got)).astype(jnp.bfloat16)


def halve(array, dim, pairing):
    keep = lax.index_in_dim(array, 0, dim, keepdims=False)
    return add(keep, across(lax.index_in_dim(array, 1, dim, keepdims=False), pairing))


def reduce_parts(halves, packed_tokens, state):
    pairs, dims = [], []
    for m, (v, w, _, _) in enumerate(ORDERS):
        pairs += [halves[2 * m], across(halves[2 * m + 1], v)]
        dims.append(w - (v < w))
    *sums, packed_tokens = add_halves(pairs, dims, (state,), (packed_tokens,))
    tokens = core_swap(packed_tokens)
    parts = []
    for m, (_, w, p, q) in enumerate(ORDERS):
        keep, send = sums[2 * m : 2 * m + 2]
        keep, send = add_halves([keep, across(send, w)], [int(p > q)])
        keep, send = add_halves([keep, across(send, p)], [0], () if m else (tokens,))
        total = wide(keep[0]) + wide(across(send[0], q))
        parts.append(total.astype(jnp.bfloat16) if m else total)
    return parts, tokens


def reduce_z(parts):
    total = parts[0]
    for m in range(1, PARTS):
        total = total + wide(z_swap(parts[m], m))
    total = total.astype(jnp.bfloat16)
    return (wide(total) + wide(z_swap(total, 7))).reshape(2, 32, COLS)


def gather_parts(rows):
    halves = []
    for m, (v, w, p, q) in enumerate(ORDERS):
        part = (z_swap(rows, m) if m else rows)[None]
        for bit, dim in ((q, 0), (p, sorted((p, q)).index(p)), (w, w - (v < w))):
            part = join(part, across(part, bit), dim)
        halves += [part, across(part, v)]
    return halves


def local(activations, output_grads, master_weights, first_moment, second_moment, next_tokens):
    low = lax.axis_index("outer") % 8 < 4
    packed, packed_acts = pack_acts(activations, output_grads)
    packed_tokens, state, packed_all = pack_rest(
        next_tokens, master_weights, first_moment, second_moment, packed_acts
    )
    halves = gradient_term(activations, core_swap(packed), output_grads, packed_all)
    got_state = z_swap(state, 7)

    parts, got_tokens = reduce_parts(halves, packed_tokens, got_state)
    gradient = reduce_z(parts)
    pairs = jnp.stack([jnp.where(low, state, got_state), jnp.where(low, got_state, state)], axis=1)
    updated = adamw_update(gradient, *pairs)
    new_master, new_first, new_second = (jnp.where(low, u[0], u[1]) for u in updated)
    rows = updated[0].astype(jnp.bfloat16).reshape(64, COLS)

    kept_weights, mine, theirs = project(next_tokens, got_tokens, gather_parts(rows))
    projection = (mine + wide(core_swap(theirs))).astype(jnp.bfloat16)
    return (new_master, new_first, new_second, kept_weights, projection)


def solution(mesh):
    placed = (
        P(("outer", "inner"), None),
        P(("outer", "inner"), None),
        P(("inner", "outer"), None),
        P(("inner", "outer"), None),
        P(("inner", "outer"), None),
        P(("outer", "inner"), None),
    )
    return jax.shard_map(
        local,
        mesh=mesh,
        in_specs=placed,
        out_specs=(
            P(("inner", "outer"), None),
            P(("inner", "outer"), None),
            P(("inner", "outer"), None),
            P("inner", None),
            P(("outer", "inner"), None),
        ),
        check_vma=False,
    )
```

```python
import functools
import itertools

import jax
import jax.numpy as jnp
from jax import lax
from jax.experimental import pallas as pl
from jax.experimental.pallas import tpu as pltpu
from jax.sharding import PartitionSpec as P

ADAM_STEP = 10
beta_first = 0.9
beta_second = 0.95
learn_rate = 0.002
decay_rate = 0.1
adam_eps = 1e-08

AXES = ("outer", "inner")
SIZES = (2, 8, 4, 2, 2)
TOK = 256
COLS = 512
HALF = 4096
BLOCK = 256
BLOCKS = 16
PARTS = 4
ROWS = 64

ORDERS = ((0, 2, 1, 3), (1, 3, 0, 2), (2, 0, 1, 3), (3, 1, 0, 2))
COUPLES = ((0, 2, 1, 3), (1, 3, 0, 2))


def moves(change):
    pairs = []
    for here in itertools.product(*(range(n) for n in SIZES)):
        source = target = 0
        for n, i, j in zip(SIZES, here, change(*here)):
            source, target = source * n + i, target * n + j
        pairs.append((source, target))
    return pairs


def paired(i, odd):
    if odd:
        return (i + 1) % 4 if i % 2 else (i - 1) % 4
    return i ^ 1


def pair(v, xh, z, y, xl, c):
    v = v ^ (2 * c)
    if v < 2:
        x = paired(xh * 2 + xl, v)
        return x // 2, z, y, x % 2, c
    return xh, z, paired(y, v - 2), xl, c


PAIRINGS = tuple(moves(functools.partial(pair, v)) for v in range(4))


def across(array, pairing):
    return lax.ppermute(array, AXES, PAIRINGS[pairing])


def around(couple, first, second):
    both = moves(lambda *here: pair(first, *pair(second, *here)))
    return [
        across(couple[1], second),
        across(couple[2], first),
        lax.ppermute(couple[3], AXES, both),
    ]


def z_swap(array, mask):
    return lax.ppermute(array, AXES, moves(lambda xh, z, y, xl, c: (xh, z ^ mask, y, xl, c)))


def core_swap(array):
    return lax.ppermute(array, AXES, moves(lambda xh, z, y, xl, c: (xh, z, y, xl, 1 - c)))


def place():
    outer, inner = lax.axis_index("outer"), lax.axis_index("inner")
    return outer // 8, outer % 8, inner // 4, (inner // 2) % 2, inner % 2


def columns_of(where, r, core):
    xh, _, y, xl, _ = where
    bits = [(r >> (3 - v)) & 1 for v in range(4)]
    a, b, c, d = (bits[v] + core * (bits[v ^ 2] - bits[v]) for v in range(4))
    to_xh, to_xl, to_y = xh ^ b, xl ^ (a ^ b), y ^ (2 * d + (c ^ d))
    block = ((to_y * 2 + to_xl) * 2 + core) * 2 + to_xh
    return pl.ds(pl.multiple_of(block * BLOCK, BLOCK), BLOCK)


def side_and_slot(m, r):
    bits = [(r >> (3 - v)) & 1 for v in range(4)]
    side = bits.pop(ORDERS[m][0])
    return side, bits[0] * 4 + bits[1] * 2 + bits[2]


def pair_starts(where, m):
    z = where[1]
    first = jnp.where(z < 4, z, 7 - z) ^ m
    return first * 32, (7 - first) * 32


ANY = pl.BlockSpec(memory_space=pl.ANY)
VMEM = pl.BlockSpec(memory_space=pltpu.VMEM)
PARAMS = pltpu.CompilerParams(vmem_limit_bytes=40 * 1024 * 1024)
WHOLE = pltpu.CompilerParams(vmem_limit_bytes=60 * 1024 * 1024)


def cost(flops, size):
    return pl.CostEstimate(flops=flops, bytes_accessed=size, transcendentals=0)


def run_all(copies):
    for copy in copies:
        copy.start()
    for copy in copies:
        copy.wait()


def theirs_of(source, packed, sems):
    where = place()
    return [
        pltpu.make_async_copy(
            source.at[:, columns_of(where, r, 1 - where[4])],
            packed.at[:, pl.ds(r * BLOCK, BLOCK)],
            sems.at[r],
        )
        for r in range(BLOCKS)
    ]


PACKED = jax.ShapeDtypeStruct((TOK, HALF), jnp.bfloat16)


DONE = jax.ShapeDtypeStruct((8, 128), jnp.float32)


def pack_acts_kernel(acts, grads, packed, done, sems):
    done[...] = jnp.zeros_like(done)
    run_all(
        theirs_of(acts, packed, sems)
        + [pltpu.make_async_copy(grads, packed.at[:, pl.ds(HALF, COLS)], sems.at[BLOCKS])]
    )


def pack_acts(acts, grads):
    return pl.pallas_call(
        pack_acts_kernel,
        out_shape=(jax.ShapeDtypeStruct((TOK, HALF + COLS), jnp.bfloat16), DONE),
        in_specs=[ANY, ANY],
        out_specs=(VMEM, VMEM),
        scratch_shapes=[pltpu.SemaphoreType.DMA((BLOCKS + 1,))],
        compiler_params=WHOLE,
        cost_estimate=cost(0, 4 << 20),
        name="pack_acts",
    )(acts, grads)


def pack_rest_kernel(tokens, master, first, second, _after, packed, state, done, sems):
    done[...] = jnp.zeros_like(done)
    run_all(
        theirs_of(tokens, packed, sems)
        + [
            pltpu.make_async_copy(source, state.at[i], sems.at[BLOCKS + i])
            for i, source in enumerate((master, first, second))
        ]
    )


def pack_rest(tokens, master, first, second, after):
    return pl.pallas_call(
        pack_rest_kernel,
        out_shape=(
            PACKED,
            jax.ShapeDtypeStruct((3, 32, COLS), jnp.float32),
            DONE,
        ),
        in_specs=[ANY] * 4 + [VMEM],
        out_specs=(VMEM, VMEM, VMEM),
        scratch_shapes=[pltpu.SemaphoreType.DMA((BLOCKS + 3,))],
        compiler_params=PARAMS,
        cost_estimate=cost(0, 5 << 20),
        name="pack_rest",
    )(tokens, master, first, second, after)


def term_kernel(acts, got, grads, _after, *refs):
    halves = refs[: 2 * PARTS]
    both, grads_both, term, sems = refs[2 * PARTS :]
    where = place()
    own, other = [], []
    for r in range(BLOCKS):
        here = pl.ds(r * BLOCK, BLOCK)
        own.append(
            pltpu.make_async_copy(
                acts.at[:, columns_of(where, r, where[4])], both.at[:TOK, here], sems.at[r]
            )
        )
        other.append(
            pltpu.make_async_copy(got.at[:, here], both.at[TOK:, here], sems.at[BLOCKS + r])
        )
    for r in range(BLOCKS):
        own[r].start()
        other[r].start()
    got_grads = pltpu.make_async_copy(
        got.at[:, pl.ds(HALF, COLS)], grads_both.at[TOK:], sems.at[2 * BLOCKS]
    )
    got_grads.start()
    grads_both[:TOK] = grads[...]
    got_grads.wait()
    starts = [pair_starts(where, m) for m in range(PARTS)]
    for r in range(BLOCKS):
        own[r].wait()
        other[r].wait()
        term[r % 2] = lax.dot_general(
            both[:, r * BLOCK : (r + 1) * BLOCK],
            grads_both[...],
            (((0,), (0,)), ((), ())),
            preferred_element_type=jnp.float32,
        ).astype(jnp.bfloat16)
        for m in range(PARTS):
            side, slot = side_and_slot(m, r)
            for j in range(2):
                halves[2 * m + side][slot, j * 32 : j * 32 + 32] = term[
                    r % 2, pl.ds(pl.multiple_of(starts[m][j], 32), 32)
                ]


def gradient_term(acts, got, grads, after):
    half = jax.ShapeDtypeStruct((8, ROWS, COLS), jnp.bfloat16)
    return pl.pallas_call(
        term_kernel,
        out_shape=(half,) * (2 * PARTS),
        in_specs=[ANY, ANY, VMEM, VMEM],
        out_specs=(VMEM,) * (2 * PARTS),
        scratch_shapes=[
            pltpu.VMEM((2 * TOK, HALF), jnp.bfloat16),
            pltpu.VMEM((2 * TOK, COLS), jnp.bfloat16),
            pltpu.VMEM((2, BLOCK, COLS), jnp.bfloat16),
            pltpu.SemaphoreType.DMA((2 * BLOCKS + 1,)),
        ],
        compiler_params=PARAMS,
        cost_estimate=cost(2 * 2 * TOK * HALF * COLS, 9 << 20),
        name="gradient_term",
    )(acts, got, grads, after)


def add_kernel(dims, n_outs, *refs):
    outs = refs[-n_outs:]
    for i, dim in enumerate(dims):
        keep, got = refs[2 * i : 2 * i + 2]
        blocks = keep.shape[0]
        inner = blocks >> (dim + 1)
        for slot in range(blocks):
            outs[2 * i + (slot // inner) % 2][slot // (2 * inner) * inner + slot % inner] = (
                keep[slot].astype(jnp.float32) + got[slot].astype(jnp.float32)
            ).astype(jnp.bfloat16)


def add_halves(pairs, dims, after=(), through=()):
    blocks = pairs[0].shape[0]
    half = jax.ShapeDtypeStruct((blocks // 2, ROWS, COLS), jnp.bfloat16)
    n, first = len(pairs), len(pairs) + len(after)
    return pl.pallas_call(
        functools.partial(add_kernel, dims, n + len(through)),
        out_shape=(half,) * n + tuple(jax.ShapeDtypeStruct(t.shape, t.dtype) for t in through),
        in_specs=[VMEM] * n + [ANY] * (len(after) + len(through)),
        out_specs=(VMEM,) * n + (ANY,) * len(through),
        input_output_aliases={first + i: n + i for i in range(len(through))},
        compiler_params=PARAMS,
        cost_estimate=cost(n * blocks << 15, n * blocks * 3 << 16),
        name="add_halves",
    )(*pairs, *after, *through)


def couple_kernel(*refs):
    outs = refs[-4 * len(COUPLES) :]
    for c, parts in enumerate(COUPLES):
        for j, m in enumerate(parts[:2]):
            keep, got = refs[2 * m : 2 * m + 2]
            for i in range(4):
                outs[4 * c + i][j] = (
                    keep[i].astype(jnp.float32) + got[i].astype(jnp.float32)
                ).astype(jnp.bfloat16)


def add_couples(pairs, after):
    block = jax.ShapeDtypeStruct((2, ROWS, COLS), jnp.bfloat16)
    return pl.pallas_call(
        couple_kernel,
        out_shape=(block,) * (4 * len(COUPLES)),
        in_specs=[VMEM] * len(pairs) + [ANY],
        out_specs=(VMEM,) * (4 * len(COUPLES)),
        compiler_params=PARAMS,
        cost_estimate=cost(1 << 19, 3 << 20),
        name="add_couples",
    )(*pairs, after)


def spread_kernel(*refs):
    for i in range(4):
        for j in range(2):
            refs[4 + j][i] = refs[i][j]


def spread(couple):
    part = jax.ShapeDtypeStruct((4, ROWS, COLS), jnp.bfloat16)
    return pl.pallas_call(
        spread_kernel,
        out_shape=(part,) * 2,
        in_specs=[VMEM] * 4,
        out_specs=(VMEM,) * 2,
        compiler_params=PARAMS,
        cost_estimate=cost(0, 1 << 20),
        name="spread",
    )(*couple)


def join_kernel(dim, here, got, both):
    blocks = here.shape[0]
    inner = blocks >> dim
    for slot in range(2 * blocks):
        source = got if (slot // inner) % 2 else here
        both[slot] = source[slot // (2 * inner) * inner + slot % inner]


def join(here, got, dim):
    blocks = here.shape[0]
    return pl.pallas_call(
        functools.partial(join_kernel, dim),
        out_shape=jax.ShapeDtypeStruct((2 * blocks, ROWS, COLS), jnp.bfloat16),
        in_specs=[VMEM, VMEM],
        out_specs=VMEM,
        compiler_params=PARAMS,
        cost_estimate=cost(0, blocks * 4 << 17),
        name="join",
    )(here, got)


STRIPE = 1024


def project_kernel(tokens, got, *refs):
    halves = refs[: 2 * PARTS]
    kept, mine, theirs, both, weights, total, sems = refs[2 * PARTS :]
    where = place()
    token_copies = [
        pltpu.make_async_copy(
            tokens.at[:, columns_of(where, r, where[4])],
            both.at[:TOK, pl.ds(r * BLOCK, BLOCK)],
            sems.at[r],
        )
        for r in range(BLOCKS)
    ]
    got_copies = [
        pltpu.make_async_copy(
            got.at[:, pl.ds(s * STRIPE, STRIPE)],
            both.at[TOK:, pl.ds(s * STRIPE, STRIPE)],
            sems.at[BLOCKS + s],
        )
        for s in range(HALF // STRIPE)
    ]
    per = STRIPE // BLOCK
    for s in range(HALF // STRIPE):
        for k in range(per):
            token_copies[s * per + k].start()
        got_copies[s].start()
    starts = [pair_starts(where, m) for m in range(PARTS)]

    def keep_block(x_hi, block):
        kept[pl.ds(pl.multiple_of(x_hi * BLOCK, BLOCK), BLOCK)] = block

    for s in range(HALF // STRIPE):
        for k in range(per):
            for m in range(PARTS):
                side, slot = side_and_slot(m, s * per + k)
                for j in range(2):
                    at = pl.ds(pl.multiple_of(k * BLOCK + starts[m][j], 32), 32)
                    weights[s % 2, at] = halves[2 * m + side][slot, j * 32 : j * 32 + 32]
            token_copies[s * per + k].wait()
        got_copies[s].wait()
        if s == 0:
            keep_block(where[0], weights[0, :BLOCK])

            @pl.when(where[4] == 1)
            def _():
                keep_block(1 - where[0], weights[0, 3 * BLOCK :])

        if s == 3:

            @pl.when(where[4] == 0)
            def _():
                keep_block(1 - where[0], weights[1, :BLOCK])

        product = jnp.dot(
            both[:, s * STRIPE : (s + 1) * STRIPE],
            weights[s % 2],
            preferred_element_type=jnp.float32,
        )
        if s == 0:
            total[...] = product
        elif s < HALF // STRIPE - 1:
            total[...] += product
        else:
            product += total[...]
            mine[...] = product[:TOK]
            theirs[...] = product[TOK:].astype(jnp.bfloat16)


def project(tokens, got, halves):
    return pl.pallas_call(
        project_kernel,
        out_shape=(
            jax.ShapeDtypeStruct((2 * BLOCK, COLS), jnp.bfloat16),
            jax.ShapeDtypeStruct((TOK, COLS), jnp.float32),
            jax.ShapeDtypeStruct((TOK, COLS), jnp.bfloat16),
        ),
        in_specs=[ANY, ANY] + [VMEM] * (2 * PARTS),
        out_specs=(VMEM,) * 3,
        scratch_shapes=[
            pltpu.VMEM((2 * TOK, HALF), jnp.bfloat16),
            pltpu.VMEM((2, STRIPE, COLS), jnp.bfloat16),
            pltpu.VMEM((2 * TOK, COLS), jnp.float32),
            pltpu.SemaphoreType.DMA((BLOCKS + HALF // STRIPE,)),
        ],
        compiler_params=PARAMS,
        cost_estimate=cost(2 * 2 * TOK * HALF * COLS, 9 << 20),
        name="project",
    )(tokens, got, *halves)


def adamw_update(gradient, master_weights, first_moment, second_moment):
    new_first = beta_first * first_moment + (1.0 - beta_first) * gradient
    new_second = beta_second * second_moment + (1.0 - beta_second) * gradient * gradient
    first_hat = new_first / (1.0 - beta_first**ADAM_STEP)
    second_hat = new_second / (1.0 - beta_second**ADAM_STEP)
    new_master = master_weights - learn_rate * (
        first_hat / (jnp.sqrt(second_hat) + adam_eps) + decay_rate * master_weights
    )
    return (new_master, new_first, new_second)


def wide(array):
    return array.astype(jnp.float32)


def add(keep, got):
    return (wide(keep) + wide(got)).astype(jnp.bfloat16)


def halve(array, dim, pairing):
    keep = lax.index_in_dim(array, 0, dim, keepdims=False)
    return add(keep, across(lax.index_in_dim(array, 1, dim, keepdims=False), pairing))


def reduce_parts(halves, packed_tokens, state):
    pairs, dims = [], []
    for m, (v, w, _, _) in enumerate(ORDERS):
        pairs += [halves[2 * m], across(halves[2 * m + 1], v)]
        dims.append(w - (v < w))
    *sums, packed_tokens = add_halves(pairs, dims, (state,), (packed_tokens,))
    tokens = core_swap(packed_tokens)
    pairs = []
    for m, (_, w, _, _) in enumerate(ORDERS):
        pairs += [sums[2 * m], across(sums[2 * m + 1], w)]
    blocks = add_couples(pairs, tokens)
    parts = [None] * PARTS
    for c, (a, b, first, second) in enumerate(COUPLES):
        couple = blocks[4 * c : 4 * c + 4]
        total = wide(couple[0])
        for got in around(couple, first, second):
            total = total + wide(got)
        parts[a], parts[b] = total[0], total[1]
    return [parts[0]] + [part.astype(jnp.bfloat16) for part in parts[1:]], tokens


def reduce_z(parts):
    total = parts[0]
    for m in range(1, PARTS):
        total = total + wide(z_swap(parts[m], m))
    total = total.astype(jnp.bfloat16)
    return (wide(total) + wide(z_swap(total, 7))).reshape(2, 32, COLS)


def gather_parts(rows):
    halves = [None] * (2 * PARTS)
    for a, b, first, second in COUPLES:
        couple = jnp.stack([z_swap(rows, m) if m else rows for m in (a, b)])
        parts = spread([couple] + around([couple] * 4, first, second))
        for m, part in zip((a, b), parts):
            v, w = ORDERS[m][:2]
            part = join(part, across(part, w), w - (v < w))
            halves[2 * m : 2 * m + 2] = [part, across(part, v)]
    return halves


def local(activations, output_grads, master_weights, first_moment, second_moment, next_tokens):
    low = lax.axis_index("outer") % 8 < 4
    packed, packed_acts = pack_acts(activations, output_grads)
    packed_tokens, state, packed_all = pack_rest(
        next_tokens, master_weights, first_moment, second_moment, packed_acts
    )
    halves = gradient_term(activations, core_swap(packed), output_grads, packed_all)
    got_state = z_swap(state, 7)

    parts, got_tokens = reduce_parts(halves, packed_tokens, got_state)
    gradient = reduce_z(parts)
    pairs = jnp.stack([jnp.where(low, state, got_state), jnp.where(low, got_state, state)], axis=1)
    updated = adamw_update(gradient, *pairs)
    new_master, new_first, new_second = (jnp.where(low, u[0], u[1]) for u in updated)
    rows = updated[0].astype(jnp.bfloat16).reshape(64, COLS)

    kept_weights, mine, theirs = project(next_tokens, got_tokens, gather_parts(rows))
    projection = (mine + wide(core_swap(theirs))).astype(jnp.bfloat16)
    return (new_master, new_first, new_second, kept_weights, projection)


def solution(mesh):
    placed = (
        P(("outer", "inner"), None),
        P(("outer", "inner"), None),
        P(("inner", "outer"), None),
        P(("inner", "outer"), None),
        P(("inner", "outer"), None),
        P(("outer", "inner"), None),
    )
    return jax.shard_map(
        local,
        mesh=mesh,
        in_specs=placed,
        out_specs=(
            P(("inner", "outer"), None),
            P(("inner", "outer"), None),
            P(("inner", "outer"), None),
            P("inner", None),
            P(("outer", "inner"), None),
        ),
        check_vma=False,
    )
```

```python
import functools
import itertools

import jax
import jax.numpy as jnp
from jax import lax
from jax.experimental import pallas as pl
from jax.experimental.pallas import tpu as pltpu
from jax.sharding import PartitionSpec as P

ADAM_STEP = 10
beta_first = 0.9
beta_second = 0.95
learn_rate = 0.002
decay_rate = 0.1
adam_eps = 1e-08

AXES = ("outer", "inner")
SIZES = (2, 8, 4, 2, 2)
TOK = 256
COLS = 512
HALF = 4096
BLOCK = 256
BLOCKS = 16
PARTS = 4
ROWS = 64

ORDERS = ((0, 2, 1, 3), (1, 3, 0, 2), (2, 0, 1, 3), (3, 1, 0, 2))
COUPLES = ((0, 2, 1, 3), (1, 3, 0, 2))


def moves(change):
    pairs = []
    for here in itertools.product(*(range(n) for n in SIZES)):
        source = target = 0
        for n, i, j in zip(SIZES, here, change(*here)):
            source, target = source * n + i, target * n + j
        pairs.append((source, target))
    return pairs


def paired(i, odd):
    if odd:
        return (i + 1) % 4 if i % 2 else (i - 1) % 4
    return i ^ 1


def pair(v, xh, z, y, xl, c):
    v = v ^ (2 * c)
    if v < 2:
        x = paired(xh * 2 + xl, v)
        return x // 2, z, y, x % 2, c
    return xh, z, paired(y, v - 2), xl, c


PAIRINGS = tuple(moves(functools.partial(pair, v)) for v in range(4))


def across(array, pairing):
    return lax.ppermute(array, AXES, PAIRINGS[pairing])


def around(couple, first, second):
    both = moves(lambda *here: pair(first, *pair(second, *here)))
    return [
        across(couple[1], second),
        across(couple[2], first),
        lax.ppermute(couple[3], AXES, both),
    ]


def z_swap(array, mask):
    return lax.ppermute(array, AXES, moves(lambda xh, z, y, xl, c: (xh, z ^ mask, y, xl, c)))


def core_swap(array):
    return lax.ppermute(array, AXES, moves(lambda xh, z, y, xl, c: (xh, z, y, xl, 1 - c)))


def place():
    outer, inner = lax.axis_index("outer"), lax.axis_index("inner")
    return outer // 8, outer % 8, inner // 4, (inner // 2) % 2, inner % 2


def columns_of(where, r, core):
    xh, _, y, xl, _ = where
    bits = [(r >> (3 - v)) & 1 for v in range(4)]
    a, b, c, d = (bits[v] + core * (bits[v ^ 2] - bits[v]) for v in range(4))
    to_xh, to_xl, to_y = xh ^ b, xl ^ (a ^ b), y ^ (2 * d + (c ^ d))
    block = ((to_y * 2 + to_xl) * 2 + core) * 2 + to_xh
    return pl.ds(pl.multiple_of(block * BLOCK, BLOCK), BLOCK)


def side_and_slot(m, r):
    bits = [(r >> (3 - v)) & 1 for v in range(4)]
    side = bits.pop(ORDERS[m][0])
    return side, bits[0] * 4 + bits[1] * 2 + bits[2]


def pair_starts(where, m):
    z = where[1]
    first = jnp.where(z < 4, z, 7 - z) ^ m
    return first * 32, (7 - first) * 32


ANY = pl.BlockSpec(memory_space=pl.ANY)
VMEM = pl.BlockSpec(memory_space=pltpu.VMEM)
PARAMS = pltpu.CompilerParams(vmem_limit_bytes=40 * 1024 * 1024)
WHOLE = pltpu.CompilerParams(vmem_limit_bytes=60 * 1024 * 1024)


def cost(flops, size):
    return pl.CostEstimate(flops=flops, bytes_accessed=size, transcendentals=0)


def run_all(copies):
    for copy in copies:
        copy.start()
    for copy in copies:
        copy.wait()


def theirs_of(source, packed, sems):
    where = place()
    return [
        pltpu.make_async_copy(
            source.at[:, columns_of(where, r, 1 - where[4])],
            packed.at[:, pl.ds(r * BLOCK, BLOCK)],
            sems.at[r],
        )
        for r in range(BLOCKS)
    ]


PACKED = jax.ShapeDtypeStruct((TOK, HALF), jnp.bfloat16)


DONE = jax.ShapeDtypeStruct((8, 128), jnp.float32)


def pack_acts_kernel(acts, grads, packed, done, sems):
    done[...] = jnp.zeros_like(done)
    run_all(
        theirs_of(acts, packed, sems)
        + [pltpu.make_async_copy(grads, packed.at[:, pl.ds(HALF, COLS)], sems.at[BLOCKS])]
    )


def pack_acts(acts, grads):
    return pl.pallas_call(
        pack_acts_kernel,
        out_shape=(jax.ShapeDtypeStruct((TOK, HALF + COLS), jnp.bfloat16), DONE),
        in_specs=[ANY, ANY],
        out_specs=(VMEM, VMEM),
        scratch_shapes=[pltpu.SemaphoreType.DMA((BLOCKS + 1,))],
        compiler_params=WHOLE,
        cost_estimate=cost(0, 4 << 20),
        name="pack_acts",
    )(acts, grads)


def pack_rest_kernel(tokens, master, first, second, _after, packed, state, done, sems):
    done[...] = jnp.zeros_like(done)
    run_all(
        theirs_of(tokens, packed, sems)
        + [
            pltpu.make_async_copy(source, state.at[i], sems.at[BLOCKS + i])
            for i, source in enumerate((master, first, second))
        ]
    )


def pack_rest(tokens, master, first, second, after):
    return pl.pallas_call(
        pack_rest_kernel,
        out_shape=(
            PACKED,
            jax.ShapeDtypeStruct((3, 32, COLS), jnp.float32),
            DONE,
        ),
        in_specs=[ANY] * 4 + [VMEM],
        out_specs=(VMEM, VMEM, VMEM),
        scratch_shapes=[pltpu.SemaphoreType.DMA((BLOCKS + 3,))],
        compiler_params=PARAMS,
        cost_estimate=cost(0, 5 << 20),
        name="pack_rest",
    )(tokens, master, first, second, after)


def term_kernel(acts, got, grads, _after, *refs):
    halves = refs[: 2 * PARTS]
    both, grads_both, term, sems = refs[2 * PARTS :]
    where = place()
    own, other = [], []
    for r in range(BLOCKS):
        here = pl.ds(r * BLOCK, BLOCK)
        own.append(
            pltpu.make_async_copy(
                acts.at[:, columns_of(where, r, where[4])], both.at[:TOK, here], sems.at[r]
            )
        )
        other.append(
            pltpu.make_async_copy(got.at[:, here], both.at[TOK:, here], sems.at[BLOCKS + r])
        )
    for r in range(BLOCKS):
        own[r].start()
        other[r].start()
    got_grads = pltpu.make_async_copy(
        got.at[:, pl.ds(HALF, COLS)], grads_both.at[TOK:], sems.at[2 * BLOCKS]
    )
    got_grads.start()
    grads_both[:TOK] = grads[...]
    got_grads.wait()
    starts = [pair_starts(where, m) for m in range(PARTS)]
    for r in range(BLOCKS):
        own[r].wait()
        other[r].wait()
        term[r % 2] = lax.dot_general(
            both[:, r * BLOCK : (r + 1) * BLOCK],
            grads_both[...],
            (((0,), (0,)), ((), ())),
            preferred_element_type=jnp.float32,
        ).astype(jnp.bfloat16)
        for m in range(PARTS):
            side, slot = side_and_slot(m, r)
            for j in range(2):
                halves[2 * m + side][slot, j * 32 : j * 32 + 32] = term[
                    r % 2, pl.ds(pl.multiple_of(starts[m][j], 32), 32)
                ]


def gradient_term(acts, got, grads, after):
    half = jax.ShapeDtypeStruct((8, ROWS, COLS), jnp.bfloat16)
    return pl.pallas_call(
        term_kernel,
        out_shape=(half,) * (2 * PARTS),
        in_specs=[ANY, ANY, VMEM, VMEM],
        out_specs=(VMEM,) * (2 * PARTS),
        scratch_shapes=[
            pltpu.VMEM((2 * TOK, HALF), jnp.bfloat16),
            pltpu.VMEM((2 * TOK, COLS), jnp.bfloat16),
            pltpu.VMEM((2, BLOCK, COLS), jnp.bfloat16),
            pltpu.SemaphoreType.DMA((2 * BLOCKS + 1,)),
        ],
        compiler_params=PARAMS,
        cost_estimate=cost(2 * 2 * TOK * HALF * COLS, 9 << 20),
        name="gradient_term",
    )(acts, got, grads, after)


def add_kernel(dims, n_outs, *refs):
    outs = refs[-n_outs:]
    for i, dim in enumerate(dims):
        keep, got = refs[2 * i : 2 * i + 2]
        blocks = keep.shape[0]
        inner = blocks >> (dim + 1)
        for slot in range(blocks):
            outs[2 * i + (slot // inner) % 2][slot // (2 * inner) * inner + slot % inner] = (
                keep[slot].astype(jnp.float32) + got[slot].astype(jnp.float32)
            ).astype(jnp.bfloat16)


def add_halves(pairs, dims, after=(), through=()):
    blocks = pairs[0].shape[0]
    half = jax.ShapeDtypeStruct((blocks // 2, ROWS, COLS), jnp.bfloat16)
    n, first = len(pairs), len(pairs) + len(after)
    return pl.pallas_call(
        functools.partial(add_kernel, dims, n + len(through)),
        out_shape=(half,) * n + tuple(jax.ShapeDtypeStruct(t.shape, t.dtype) for t in through),
        in_specs=[VMEM] * n + [ANY] * (len(after) + len(through)),
        out_specs=(VMEM,) * n + (ANY,) * len(through),
        input_output_aliases={first + i: n + i for i in range(len(through))},
        compiler_params=PARAMS,
        cost_estimate=cost(n * blocks << 15, n * blocks * 3 << 16),
        name="add_halves",
    )(*pairs, *after, *through)


def couple_kernel(*refs):
    outs = refs[-4 * len(COUPLES) :]
    for c, parts in enumerate(COUPLES):
        for j, m in enumerate(parts[:2]):
            keep, got = refs[2 * m : 2 * m + 2]
            for i in range(4):
                outs[4 * c + i][j] = (
                    keep[i].astype(jnp.float32) + got[i].astype(jnp.float32)
                ).astype(jnp.bfloat16)


def add_couples(pairs, after):
    block = jax.ShapeDtypeStruct((2, ROWS, COLS), jnp.bfloat16)
    return pl.pallas_call(
        couple_kernel,
        out_shape=(block,) * (4 * len(COUPLES)),
        in_specs=[VMEM] * len(pairs) + [ANY],
        out_specs=(VMEM,) * (4 * len(COUPLES)),
        compiler_params=PARAMS,
        cost_estimate=cost(1 << 19, 3 << 20),
        name="add_couples",
    )(*pairs, after)


def join_kernel(dim, here, got, both):
    blocks = here.shape[0]
    inner = blocks >> dim
    for slot in range(2 * blocks):
        source = got if (slot // inner) % 2 else here
        both[slot] = source[slot // (2 * inner) * inner + slot % inner]


def join(here, got, dim):
    blocks = here.shape[0]
    return pl.pallas_call(
        functools.partial(join_kernel, dim),
        out_shape=jax.ShapeDtypeStruct((2 * blocks, ROWS, COLS), jnp.bfloat16),
        in_specs=[VMEM, VMEM],
        out_specs=VMEM,
        compiler_params=PARAMS,
        cost_estimate=cost(0, blocks * 4 << 17),
        name="join",
    )(here, got)


STRIPE = 1024


def project_kernel(tokens, got, *refs):
    halves = refs[: 2 * PARTS]
    kept, mine, theirs, both, weights, total, sems = refs[2 * PARTS :]
    where = place()
    token_copies = [
        pltpu.make_async_copy(
            tokens.at[:, columns_of(where, r, where[4])],
            both.at[:TOK, pl.ds(r * BLOCK, BLOCK)],
            sems.at[r],
        )
        for r in range(BLOCKS)
    ]
    got_copies = [
        pltpu.make_async_copy(
            got.at[:, pl.ds(s * STRIPE, STRIPE)],
            both.at[TOK:, pl.ds(s * STRIPE, STRIPE)],
            sems.at[BLOCKS + s],
        )
        for s in range(HALF // STRIPE)
    ]
    per = STRIPE // BLOCK
    for s in range(HALF // STRIPE):
        for k in range(per):
            token_copies[s * per + k].start()
        got_copies[s].start()
    starts = [pair_starts(where, m) for m in range(PARTS)]

    def keep_block(x_hi, block):
        kept[pl.ds(pl.multiple_of(x_hi * BLOCK, BLOCK), BLOCK)] = block

    for s in range(HALF // STRIPE):
        for k in range(per):
            for m in range(PARTS):
                side, slot = side_and_slot(m, s * per + k)
                for j in range(2):
                    at = pl.ds(pl.multiple_of(k * BLOCK + starts[m][j], 32), 32)
                    weights[s % 2, at] = halves[2 * m + side][slot, j * 32 : j * 32 + 32]
            token_copies[s * per + k].wait()
        got_copies[s].wait()
        if s == 0:
            keep_block(where[0], weights[0, :BLOCK])

            @pl.when(where[4] == 1)
            def _():
                keep_block(1 - where[0], weights[0, 3 * BLOCK :])

        if s == 3:

            @pl.when(where[4] == 0)
            def _():
                keep_block(1 - where[0], weights[1, :BLOCK])

        product = jnp.dot(
            both[:, s * STRIPE : (s + 1) * STRIPE],
            weights[s % 2],
            preferred_element_type=jnp.float32,
        )
        if s == 0:
            total[...] = product
        elif s < HALF // STRIPE - 1:
            total[...] += product
        else:
            product += total[...]
            mine[...] = product[:TOK]
            theirs[...] = product[TOK:].astype(jnp.bfloat16)


def project(tokens, got, halves):
    return pl.pallas_call(
        project_kernel,
        out_shape=(
            jax.ShapeDtypeStruct((2 * BLOCK, COLS), jnp.bfloat16),
            jax.ShapeDtypeStruct((TOK, COLS), jnp.float32),
            jax.ShapeDtypeStruct((TOK, COLS), jnp.bfloat16),
        ),
        in_specs=[ANY, ANY] + [VMEM] * (2 * PARTS),
        out_specs=(VMEM,) * 3,
        scratch_shapes=[
            pltpu.VMEM((2 * TOK, HALF), jnp.bfloat16),
            pltpu.VMEM((2, STRIPE, COLS), jnp.bfloat16),
            pltpu.VMEM((2 * TOK, COLS), jnp.float32),
            pltpu.SemaphoreType.DMA((BLOCKS + HALF // STRIPE,)),
        ],
        compiler_params=PARAMS,
        cost_estimate=cost(2 * 2 * TOK * HALF * COLS, 9 << 20),
        name="project",
    )(tokens, got, *halves)


def adamw_update(gradient, master_weights, first_moment, second_moment):
    new_first = beta_first * first_moment + (1.0 - beta_first) * gradient
    new_second = beta_second * second_moment + (1.0 - beta_second) * gradient * gradient
    first_hat = new_first / (1.0 - beta_first**ADAM_STEP)
    second_hat = new_second / (1.0 - beta_second**ADAM_STEP)
    new_master = master_weights - learn_rate * (
        first_hat / (jnp.sqrt(second_hat) + adam_eps) + decay_rate * master_weights
    )
    return (new_master, new_first, new_second)


def wide(array):
    return array.astype(jnp.float32)


def add(keep, got):
    return (wide(keep) + wide(got)).astype(jnp.bfloat16)


def halve(array, dim, pairing):
    keep = lax.index_in_dim(array, 0, dim, keepdims=False)
    return add(keep, across(lax.index_in_dim(array, 1, dim, keepdims=False), pairing))


def reduce_parts(halves, packed_tokens, state):
    pairs, dims = [], []
    for m, (v, w, _, _) in enumerate(ORDERS):
        pairs += [halves[2 * m], across(halves[2 * m + 1], v)]
        dims.append(w - (v < w))
    *sums, packed_tokens = add_halves(pairs, dims, (state,), (packed_tokens,))
    tokens = core_swap(packed_tokens)
    pairs = []
    for m, (_, w, _, _) in enumerate(ORDERS):
        pairs += [sums[2 * m], across(sums[2 * m + 1], w)]
    blocks = add_couples(pairs, tokens)
    parts = [None] * PARTS
    for c, (a, b, first, second) in enumerate(COUPLES):
        couple = blocks[4 * c : 4 * c + 4]
        total = wide(couple[0])
        for got in around(couple, first, second):
            total = total + wide(got)
        parts[a], parts[b] = total[0], total[1]
    return [parts[0]] + [part.astype(jnp.bfloat16) for part in parts[1:]], tokens


def reduce_z(parts):
    total = parts[0]
    for m in range(1, PARTS):
        total = total + wide(z_swap(parts[m], m))
    total = total.astype(jnp.bfloat16)
    return (wide(total) + wide(z_swap(total, 7))).reshape(2, 32, COLS)


def gather_parts(rows):
    halves = []
    for m, (v, w, p, q) in enumerate(ORDERS):
        p, q = (q, p) if m in (2, 3) else (p, q)
        part = (z_swap(rows, m) if m else rows)[None]
        for bit, dim in ((q, 0), (p, int(p > q)), (w, w - (v < w))):
            part = join(part, across(part, bit), dim)
        halves += [part, across(part, v)]
    return halves


def local(activations, output_grads, master_weights, first_moment, second_moment, next_tokens):
    low = lax.axis_index("outer") % 8 < 4
    packed, packed_acts = pack_acts(activations, output_grads)
    packed_tokens, state, packed_all = pack_rest(
        next_tokens, master_weights, first_moment, second_moment, packed_acts
    )
    halves = gradient_term(activations, core_swap(packed), output_grads, packed_all)
    got_state = z_swap(state, 7)

    parts, got_tokens = reduce_parts(halves, packed_tokens, got_state)
    gradient = reduce_z(parts)
    pairs = jnp.stack([jnp.where(low, state, got_state), jnp.where(low, got_state, state)], axis=1)
    updated = adamw_update(gradient, *pairs)
    new_master, new_first, new_second = (jnp.where(low, u[0], u[1]) for u in updated)
    rows = updated[0].astype(jnp.bfloat16).reshape(64, COLS)

    kept_weights, mine, theirs = project(next_tokens, got_tokens, gather_parts(rows))
    projection = (mine + wide(core_swap(theirs))).astype(jnp.bfloat16)
    return (new_master, new_first, new_second, kept_weights, projection)


def solution(mesh):
    placed = (
        P(("outer", "inner"), None),
        P(("outer", "inner"), None),
        P(("inner", "outer"), None),
        P(("inner", "outer"), None),
        P(("inner", "outer"), None),
        P(("outer", "inner"), None),
    )
    return jax.shard_map(
        local,
        mesh=mesh,
        in_specs=placed,
        out_specs=(
            P(("inner", "outer"), None),
            P(("inner", "outer"), None),
            P(("inner", "outer"), None),
            P("inner", None),
            P(("outer", "inner"), None),
        ),
        check_vma=False,
    )
```

```python
import functools
import itertools

import jax
import jax.numpy as jnp
from jax import lax
from jax.experimental import pallas as pl
from jax.experimental.pallas import tpu as pltpu
from jax.sharding import PartitionSpec as P

ADAM_STEP = 10
beta_first = 0.9
beta_second = 0.95
learn_rate = 0.002
decay_rate = 0.1
adam_eps = 1e-08

AXES = ("outer", "inner")
SIZES = (2, 8, 4, 2, 2)
TOK = 256
COLS = 512
HALF = 4096
BLOCK = 256
BLOCKS = 16
PARTS = 4
ROWS = 64

ORDERS = ((0, 2, 1, 3), (1, 3, 0, 2), (2, 0, 3, 1), (3, 1, 2, 0))


def moves(change):
    pairs = []
    for here in itertools.product(*(range(n) for n in SIZES)):
        source = target = 0
        for n, i, j in zip(SIZES, here, change(*here)):
            source, target = source * n + i, target * n + j
        pairs.append((source, target))
    return pairs


def paired(i, odd):
    if odd:
        return (i + 1) % 4 if i % 2 else (i - 1) % 4
    return i ^ 1


def pair(v, xh, z, y, xl, c):
    v = v ^ (2 * c)
    if v < 2:
        x = paired(xh * 2 + xl, v)
        return x // 2, z, y, x % 2, c
    return xh, z, paired(y, v - 2), xl, c


PAIRINGS = tuple(moves(functools.partial(pair, v)) for v in range(4))


def across(array, pairing):
    return lax.ppermute(array, AXES, PAIRINGS[pairing])


def z_swap(array, mask):
    return lax.ppermute(array, AXES, moves(lambda xh, z, y, xl, c: (xh, z ^ mask, y, xl, c)))


def core_swap(array):
    return lax.ppermute(array, AXES, moves(lambda xh, z, y, xl, c: (xh, z, y, xl, 1 - c)))


def place():
    outer, inner = lax.axis_index("outer"), lax.axis_index("inner")
    return outer // 8, outer % 8, inner // 4, (inner // 2) % 2, inner % 2


def columns_of(where, r, core):
    xh, _, y, xl, _ = where
    bits = [(r >> (3 - v)) & 1 for v in range(4)]
    a, b, c, d = (bits[v] + core * (bits[v ^ 2] - bits[v]) for v in range(4))
    to_xh, to_xl, to_y = xh ^ b, xl ^ (a ^ b), y ^ (2 * d + (c ^ d))
    block = ((to_y * 2 + to_xl) * 2 + core) * 2 + to_xh
    return pl.ds(pl.multiple_of(block * BLOCK, BLOCK), BLOCK)


def side_and_slot(m, r):
    bits = [(r >> (3 - v)) & 1 for v in range(4)]
    side = bits.pop(ORDERS[m][0])
    return side, bits[0] * 4 + bits[1] * 2 + bits[2]


def pair_starts(where, m):
    z = where[1]
    first = jnp.where(z < 4, z, 7 - z) ^ m
    return first * 32, (7 - first) * 32


ANY = pl.BlockSpec(memory_space=pl.ANY)
VMEM = pl.BlockSpec(memory_space=pltpu.VMEM)
PARAMS = pltpu.CompilerParams(vmem_limit_bytes=40 * 1024 * 1024)
WHOLE = pltpu.CompilerParams(vmem_limit_bytes=60 * 1024 * 1024)


def cost(flops, size):
    return pl.CostEstimate(flops=flops, bytes_accessed=size, transcendentals=0)


def run_all(copies):
    for copy in copies:
        copy.start()
    for copy in copies:
        copy.wait()


def theirs_of(source, packed, sems, pieces=1):
    where = place()
    rows = TOK // pieces
    return [
        pltpu.make_async_copy(
            source.at[pl.ds(i * rows, rows), columns_of(where, r, 1 - where[4])],
            packed.at[pl.ds(i * rows, rows), pl.ds(r * BLOCK, BLOCK)],
            sems.at[r * pieces + i],
        )
        for r in range(BLOCKS)
        for i in range(pieces)
    ]


PACKED = jax.ShapeDtypeStruct((TOK, HALF), jnp.bfloat16)


DONE = jax.ShapeDtypeStruct((8, 128), jnp.float32)


PIECES = 1


def pack_acts_kernel(acts, grads, packed, done, sems):
    done[...] = jnp.zeros_like(done)
    run_all(
        theirs_of(acts, packed, sems, PIECES)
        + [pltpu.make_async_copy(grads, packed.at[:, pl.ds(HALF, COLS)], sems.at[BLOCKS * PIECES])]
    )


def pack_acts(acts, grads):
    return pl.pallas_call(
        pack_acts_kernel,
        out_shape=(jax.ShapeDtypeStruct((TOK, HALF + COLS), jnp.bfloat16), DONE),
        in_specs=[ANY, ANY],
        out_specs=(VMEM, VMEM),
        scratch_shapes=[pltpu.SemaphoreType.DMA((BLOCKS * PIECES + 1,))],
        compiler_params=WHOLE,
        cost_estimate=cost(0, 4 << 20),
        name="pack_acts",
    )(acts, grads)


def pack_rest_kernel(tokens, master, first, second, _after, packed, state, done, sems):
    done[...] = jnp.zeros_like(done)
    run_all(
        theirs_of(tokens, packed, sems)
        + [
            pltpu.make_async_copy(source, state.at[i], sems.at[BLOCKS + i])
            for i, source in enumerate((master, first, second))
        ]
    )


def pack_rest(tokens, master, first, second, after):
    return pl.pallas_call(
        pack_rest_kernel,
        out_shape=(
            PACKED,
            jax.ShapeDtypeStruct((3, 32, COLS), jnp.float32),
            DONE,
        ),
        in_specs=[ANY] * 4 + [VMEM],
        out_specs=(VMEM, VMEM, VMEM),
        scratch_shapes=[pltpu.SemaphoreType.DMA((BLOCKS + 3,))],
        compiler_params=PARAMS,
        cost_estimate=cost(0, 5 << 20),
        name="pack_rest",
    )(tokens, master, first, second, after)


def term_kernel(acts, got, grads, _after, *refs):
    halves = refs[: 2 * PARTS]
    both, grads_both, term, sems = refs[2 * PARTS :]
    where = place()
    own, other = [], []
    for r in range(BLOCKS):
        here = pl.ds(r * BLOCK, BLOCK)
        own.append(
            pltpu.make_async_copy(
                acts.at[:, columns_of(where, r, where[4])], both.at[:TOK, here], sems.at[r]
            )
        )
        other.append(
            pltpu.make_async_copy(got.at[:, here], both.at[TOK:, here], sems.at[BLOCKS + r])
        )
    for r in range(BLOCKS):
        own[r].start()
        other[r].start()
    got_grads = pltpu.make_async_copy(
        got.at[:, pl.ds(HALF, COLS)], grads_both.at[TOK:], sems.at[2 * BLOCKS]
    )
    got_grads.start()
    grads_both[:TOK] = grads[...]
    got_grads.wait()
    starts = [pair_starts(where, m) for m in range(PARTS)]
    for r in range(BLOCKS):
        own[r].wait()
        other[r].wait()
        term[r % 2] = lax.dot_general(
            both[:, r * BLOCK : (r + 1) * BLOCK],
            grads_both[...],
            (((0,), (0,)), ((), ())),
            preferred_element_type=jnp.float32,
        ).astype(jnp.bfloat16)
        for m in range(PARTS):
            side, slot = side_and_slot(m, r)
            for j in range(2):
                halves[2 * m + side][slot, j * 32 : j * 32 + 32] = term[
                    r % 2, pl.ds(pl.multiple_of(starts[m][j], 32), 32)
                ]


def gradient_term(acts, got, grads, after):
    half = jax.ShapeDtypeStruct((8, ROWS, COLS), jnp.bfloat16)
    return pl.pallas_call(
        term_kernel,
        out_shape=(half,) * (2 * PARTS),
        in_specs=[ANY, ANY, VMEM, VMEM],
        out_specs=(VMEM,) * (2 * PARTS),
        scratch_shapes=[
            pltpu.VMEM((2 * TOK, HALF), jnp.bfloat16),
            pltpu.VMEM((2 * TOK, COLS), jnp.bfloat16),
            pltpu.VMEM((2, BLOCK, COLS), jnp.bfloat16),
            pltpu.SemaphoreType.DMA((2 * BLOCKS + 1,)),
        ],
        compiler_params=PARAMS,
        cost_estimate=cost(2 * 2 * TOK * HALF * COLS, 9 << 20),
        name="gradient_term",
    )(acts, got, grads, after)


def add_kernel(dims, n_outs, *refs):
    outs = refs[-n_outs:]
    for i, dim in enumerate(dims):
        keep, got = refs[2 * i : 2 * i + 2]
        blocks = keep.shape[0]
        inner = blocks >> (dim + 1)
        for slot in range(blocks):
            outs[2 * i + (slot // inner) % 2][slot // (2 * inner) * inner + slot % inner] = (
                keep[slot].astype(jnp.float32) + got[slot].astype(jnp.float32)
            ).astype(jnp.bfloat16)


def add_halves(pairs, dims, after=(), through=()):
    blocks = pairs[0].shape[0]
    half = jax.ShapeDtypeStruct((blocks // 2, ROWS, COLS), jnp.bfloat16)
    n, first = len(pairs), len(pairs) + len(after)
    return pl.pallas_call(
        functools.partial(add_kernel, dims, n + len(through)),
        out_shape=(half,) * n + tuple(jax.ShapeDtypeStruct(t.shape, t.dtype) for t in through),
        in_specs=[VMEM] * n + [ANY] * (len(after) + len(through)),
        out_specs=(VMEM,) * n + (ANY,) * len(through),
        input_output_aliases={first + i: n + i for i in range(len(through))},
        compiler_params=PARAMS,
        cost_estimate=cost(n * blocks << 15, n * blocks * 3 << 16),
        name="add_halves",
    )(*pairs, *after, *through)


def join_kernel(dim, here, got, both):
    blocks = here.shape[0]
    inner = blocks >> dim
    for slot in range(2 * blocks):
        source = got if (slot // inner) % 2 else here
        both[slot] = source[slot // (2 * inner) * inner + slot % inner]


def join(here, got, dim):
    blocks = here.shape[0]
    return pl.pallas_call(
        functools.partial(join_kernel, dim),
        out_shape=jax.ShapeDtypeStruct((2 * blocks, ROWS, COLS), jnp.bfloat16),
        in_specs=[VMEM, VMEM],
        out_specs=VMEM,
        compiler_params=PARAMS,
        cost_estimate=cost(0, blocks * 4 << 17),
        name="join",
    )(here, got)


STRIPE = 1024


def stage_kernel(tokens, got, *refs):
    both, sems = refs[-2:]
    where = place()
    run_all(
        [
            pltpu.make_async_copy(
                tokens.at[:, columns_of(where, r, where[4])],
                both.at[pl.ds(0, TOK), pl.ds(r * BLOCK, BLOCK)],
                sems.at[r],
            )
            for r in range(BLOCKS)
        ]
        + [pltpu.make_async_copy(got, both.at[pl.ds(TOK, TOK)], sems.at[BLOCKS])]
    )


def stage(tokens, got, after):
    return pl.pallas_call(
        stage_kernel,
        out_shape=jax.ShapeDtypeStruct((2 * TOK, HALF), jnp.bfloat16),
        in_specs=[ANY, ANY] + [VMEM] * len(after),
        out_specs=VMEM,
        scratch_shapes=[pltpu.SemaphoreType.DMA((BLOCKS + 1,))],
        compiler_params=PARAMS,
        cost_estimate=cost(0, 8 << 20),
        name="stage",
    )(tokens, got, *after)


def project_kernel(both, *refs):
    halves = refs[: 2 * PARTS]
    kept, mine, theirs, weights, total = refs[2 * PARTS :]
    where = place()
    per = STRIPE // BLOCK
    starts = [pair_starts(where, m) for m in range(PARTS)]

    def keep_block(x_hi, block):
        kept[pl.ds(pl.multiple_of(x_hi * BLOCK, BLOCK), BLOCK)] = block

    for s in range(HALF // STRIPE):
        for k in range(per):
            for m in range(PARTS):
                side, slot = side_and_slot(m, s * per + k)
                for j in range(2):
                    at = pl.ds(pl.multiple_of(k * BLOCK + starts[m][j], 32), 32)
                    weights[s % 2, at] = halves[2 * m + side][slot, j * 32 : j * 32 + 32]
        if s == 0:
            keep_block(where[0], weights[0, :BLOCK])

            @pl.when(where[4] == 1)
            def _():
                keep_block(1 - where[0], weights[0, 3 * BLOCK :])

        if s == 3:

            @pl.when(where[4] == 0)
            def _():
                keep_block(1 - where[0], weights[1, :BLOCK])

        product = jnp.dot(
            both[:, s * STRIPE : (s + 1) * STRIPE],
            weights[s % 2],
            preferred_element_type=jnp.float32,
        )
        if s == 0:
            total[...] = product
        elif s < HALF // STRIPE - 1:
            total[...] += product
        else:
            product += total[...]
            mine[...] = product[:TOK]
            theirs[...] = product[TOK:].astype(jnp.bfloat16)


def project(both, halves):
    return pl.pallas_call(
        project_kernel,
        out_shape=(
            jax.ShapeDtypeStruct((2 * BLOCK, COLS), jnp.bfloat16),
            jax.ShapeDtypeStruct((TOK, COLS), jnp.float32),
            jax.ShapeDtypeStruct((TOK, COLS), jnp.bfloat16),
        ),
        in_specs=[VMEM] * (1 + 2 * PARTS),
        out_specs=(VMEM,) * 3,
        scratch_shapes=[
            pltpu.VMEM((2, STRIPE, COLS), jnp.bfloat16),
            pltpu.VMEM((2 * TOK, COLS), jnp.float32),
        ],
        compiler_params=PARAMS,
        cost_estimate=cost(2 * 2 * TOK * HALF * COLS, 9 << 20),
        name="project",
    )(both, *halves)


def adamw_update(gradient, master_weights, first_moment, second_moment):
    new_first = beta_first * first_moment + (1.0 - beta_first) * gradient
    new_second = beta_second * second_moment + (1.0 - beta_second) * gradient * gradient
    first_hat = new_first / (1.0 - beta_first**ADAM_STEP)
    second_hat = new_second / (1.0 - beta_second**ADAM_STEP)
    new_master = master_weights - learn_rate * (
        first_hat / (jnp.sqrt(second_hat) + adam_eps) + decay_rate * master_weights
    )
    return (new_master, new_first, new_second)


def wide(array):
    return array.astype(jnp.float32)


def add(keep, got):
    return (wide(keep) + wide(got)).astype(jnp.bfloat16)


def halve(array, dim, pairing):
    keep = lax.index_in_dim(array, 0, dim, keepdims=False)
    return add(keep, across(lax.index_in_dim(array, 1, dim, keepdims=False), pairing))


def reduce_parts(halves, packed_tokens, state):
    pairs, dims = [], []
    for m, (v, w, _, _) in enumerate(ORDERS):
        pairs += [halves[2 * m], across(halves[2 * m + 1], v)]
        dims.append(w - (v < w))
    *sums, packed_tokens = add_halves(pairs, dims, (state,), (packed_tokens,))
    tokens = core_swap(packed_tokens)
    parts = []
    for m, (_, w, p, q) in enumerate(ORDERS):
        keep, send = sums[2 * m : 2 * m + 2]
        keep, send = add_halves([keep, across(send, w)], [int(p > q)])
        keep, send = add_halves([keep, across(send, p)], [0], () if m else (tokens,))
        total = wide(keep[0]) + wide(across(send[0], q))
        parts.append(total.astype(jnp.bfloat16) if m else total)
    return parts, tokens


def reduce_z(parts):
    total = parts[0]
    for m in range(1, PARTS):
        total = total + wide(z_swap(parts[m], m))
    total = total.astype(jnp.bfloat16)
    return (wide(total) + wide(z_swap(total, 7))).reshape(2, 32, COLS)


def gather_parts(rows):
    halves = []
    for m, (v, w, p, q) in enumerate(ORDERS):
        part = (z_swap(rows, m) if m else rows)[None]
        for bit, dim in ((q, 0), (p, sorted((p, q)).index(p)), (w, w - (v < w))):
            part = join(part, across(part, bit), dim)
        halves += [part, across(part, v)]
    return halves


def local(activations, output_grads, master_weights, first_moment, second_moment, next_tokens):
    low = lax.axis_index("outer") % 8 < 4
    packed, packed_acts = pack_acts(activations, output_grads)
    packed_tokens, state, packed_all = pack_rest(
        next_tokens, master_weights, first_moment, second_moment, packed_acts
    )
    halves = gradient_term(activations, core_swap(packed), output_grads, packed_all)
    got_state = z_swap(state, 7)

    parts, got_tokens = reduce_parts(halves, packed_tokens, got_state)
    gradient = reduce_z(parts)
    pairs = jnp.stack([jnp.where(low, state, got_state), jnp.where(low, got_state, state)], axis=1)
    updated = adamw_update(gradient, *pairs)
    new_master, new_first, new_second = (jnp.where(low, u[0], u[1]) for u in updated)
    rows = updated[0].astype(jnp.bfloat16).reshape(64, COLS)

    gathered = gather_parts(rows)
    both = stage(next_tokens, got_tokens, gathered[::2])
    kept_weights, mine, theirs = project(both, gathered)
    projection = (mine + wide(core_swap(theirs))).astype(jnp.bfloat16)
    return (new_master, new_first, new_second, kept_weights, projection)


def solution(mesh):
    placed = (
        P(("outer", "inner"), None),
        P(("outer", "inner"), None),
        P(("inner", "outer"), None),
        P(("inner", "outer"), None),
        P(("inner", "outer"), None),
        P(("outer", "inner"), None),
    )
    return jax.shard_map(
        local,
        mesh=mesh,
        in_specs=placed,
        out_specs=(
            P(("inner", "outer"), None),
            P(("inner", "outer"), None),
            P(("inner", "outer"), None),
            P("inner", None),
            P(("outer", "inner"), None),
        ),
        check_vma=False,
    )
```

```python
import functools
import itertools

import jax
import jax.numpy as jnp
from jax import lax
from jax.experimental import pallas as pl
from jax.experimental.pallas import tpu as pltpu
from jax.sharding import PartitionSpec as P

ADAM_STEP = 10
beta_first = 0.9
beta_second = 0.95
learn_rate = 0.002
decay_rate = 0.1
adam_eps = 1e-08

AXES = ("outer", "inner")
SIZES = (2, 8, 4, 2, 2)
TOK = 256
COLS = 512
HALF = 4096
BLOCK = 256
BLOCKS = 16
PARTS = 4
ROWS = 64

ORDERS = ((0, 2, 1, 3), (1, 3, 0, 2), (2, 0, 3, 1), (3, 1, 2, 0))


def moves(change):
    pairs = []
    for here in itertools.product(*(range(n) for n in SIZES)):
        source = target = 0
        for n, i, j in zip(SIZES, here, change(*here)):
            source, target = source * n + i, target * n + j
        pairs.append((source, target))
    return pairs


def paired(i, odd):
    if odd:
        return (i + 1) % 4 if i % 2 else (i - 1) % 4
    return i ^ 1


def pair(v, xh, z, y, xl, c):
    v = v ^ (2 * c)
    if v < 2:
        x = paired(xh * 2 + xl, v)
        return x // 2, z, y, x % 2, c
    return xh, z, paired(y, v - 2), xl, c


PAIRINGS = tuple(moves(functools.partial(pair, v)) for v in range(4))


def across(array, pairing):
    return lax.ppermute(array, AXES, PAIRINGS[pairing])


def z_swap(array, mask):
    return lax.ppermute(array, AXES, moves(lambda xh, z, y, xl, c: (xh, z ^ mask, y, xl, c)))


def core_swap(array):
    return lax.ppermute(array, AXES, moves(lambda xh, z, y, xl, c: (xh, z, y, xl, 1 - c)))


def place():
    outer, inner = lax.axis_index("outer"), lax.axis_index("inner")
    return outer // 8, outer % 8, inner // 4, (inner // 2) % 2, inner % 2


def columns_of(where, r, core):
    xh, _, y, xl, _ = where
    bits = [(r >> (3 - v)) & 1 for v in range(4)]
    a, b, c, d = (bits[v] + core * (bits[v ^ 2] - bits[v]) for v in range(4))
    to_xh, to_xl, to_y = xh ^ b, xl ^ (a ^ b), y ^ (2 * d + (c ^ d))
    block = ((to_y * 2 + to_xl) * 2 + core) * 2 + to_xh
    return pl.ds(pl.multiple_of(block * BLOCK, BLOCK), BLOCK)


def side_and_slot(m, r):
    bits = [(r >> (3 - v)) & 1 for v in range(4)]
    side = bits.pop(ORDERS[m][0])
    return side, bits[0] * 4 + bits[1] * 2 + bits[2]


def pair_starts(where, m):
    z = where[1]
    first = jnp.where(z < 4, z, 7 - z) ^ m
    return first * 32, (7 - first) * 32


ANY = pl.BlockSpec(memory_space=pl.ANY)
VMEM = pl.BlockSpec(memory_space=pltpu.VMEM)
PARAMS = pltpu.CompilerParams(vmem_limit_bytes=40 * 1024 * 1024)


def cost(flops, size):
    return pl.CostEstimate(flops=flops, bytes_accessed=size, transcendentals=0)


def run_all(copies):
    for copy in copies:
        copy.start()
    for copy in copies:
        copy.wait()


def theirs_of(source, packed, sems, pieces=1):
    where = place()
    rows = TOK // pieces
    return [
        pltpu.make_async_copy(
            source.at[pl.ds(i * rows, rows), columns_of(where, r, 1 - where[4])],
            packed.at[pl.ds(i * rows, rows), pl.ds(r * BLOCK, BLOCK)],
            sems.at[r * pieces + i],
        )
        for r in range(BLOCKS)
        for i in range(pieces)
    ]


PACKED = jax.ShapeDtypeStruct((TOK, HALF), jnp.bfloat16)


DONE = jax.ShapeDtypeStruct((8, 128), jnp.float32)


PIECES = 1


def pack_acts_kernel(acts, grads, packed, done, sems):
    done[...] = jnp.zeros_like(done)
    run_all(
        theirs_of(acts, packed, sems, PIECES)
        + [pltpu.make_async_copy(grads, packed.at[:, pl.ds(HALF, COLS)], sems.at[BLOCKS * PIECES])]
    )


def pack_acts(acts, grads):
    return pl.pallas_call(
        pack_acts_kernel,
        out_shape=(jax.ShapeDtypeStruct((TOK, HALF + COLS), jnp.bfloat16), DONE),
        in_specs=[ANY, ANY],
        out_specs=(VMEM, VMEM),
        scratch_shapes=[pltpu.SemaphoreType.DMA((BLOCKS * PIECES + 1,))],
        compiler_params=PARAMS,
        cost_estimate=cost(0, 4 << 20),
        name="pack_acts",
    )(acts, grads)


def pack_rest_kernel(tokens, master, first, second, _after, packed, state, done, sems):
    done[...] = jnp.zeros_like(done)
    run_all(
        theirs_of(tokens, packed, sems)
        + [
            pltpu.make_async_copy(source, state.at[i], sems.at[BLOCKS + i])
            for i, source in enumerate((master, first, second))
        ]
    )


def pack_rest(tokens, master, first, second, after):
    return pl.pallas_call(
        pack_rest_kernel,
        out_shape=(
            PACKED,
            jax.ShapeDtypeStruct((3, 32, COLS), jnp.float32),
            DONE,
        ),
        in_specs=[ANY] * 4 + [VMEM],
        out_specs=(VMEM, VMEM, VMEM),
        scratch_shapes=[pltpu.SemaphoreType.DMA((BLOCKS + 3,))],
        compiler_params=PARAMS,
        cost_estimate=cost(0, 5 << 20),
        name="pack_rest",
    )(tokens, master, first, second, after)


def term_kernel(acts, got, grads, _after, *refs):
    halves = refs[: 2 * PARTS]
    both, grads_both, term, sems = refs[2 * PARTS :]
    where = place()
    own, other = [], []
    for r in range(BLOCKS):
        here = pl.ds(r * BLOCK, BLOCK)
        own.append(
            pltpu.make_async_copy(
                acts.at[:, columns_of(where, r, where[4])], both.at[:TOK, here], sems.at[r]
            )
        )
        other.append(
            pltpu.make_async_copy(got.at[:, here], both.at[TOK:, here], sems.at[BLOCKS + r])
        )
    for r in range(BLOCKS):
        own[r].start()
        other[r].start()
    got_grads = pltpu.make_async_copy(
        got.at[:, pl.ds(HALF, COLS)], grads_both.at[TOK:], sems.at[2 * BLOCKS]
    )
    got_grads.start()
    grads_both[:TOK] = grads[...]
    got_grads.wait()
    starts = [pair_starts(where, m) for m in range(PARTS)]
    for r in range(BLOCKS):
        own[r].wait()
        other[r].wait()
        term[r % 2] = lax.dot_general(
            both[:, r * BLOCK : (r + 1) * BLOCK],
            grads_both[...],
            (((0,), (0,)), ((), ())),
            preferred_element_type=jnp.float32,
        ).astype(jnp.bfloat16)
        for m in range(PARTS):
            side, slot = side_and_slot(m, r)
            for j in range(2):
                halves[2 * m + side][slot, j * 32 : j * 32 + 32] = term[
                    r % 2, pl.ds(pl.multiple_of(starts[m][j], 32), 32)
                ]


def gradient_term(acts, got, grads, after):
    half = jax.ShapeDtypeStruct((8, ROWS, COLS), jnp.bfloat16)
    return pl.pallas_call(
        term_kernel,
        out_shape=(half,) * (2 * PARTS),
        in_specs=[ANY, ANY, VMEM, VMEM],
        out_specs=(VMEM,) * (2 * PARTS),
        scratch_shapes=[
            pltpu.VMEM((2 * TOK, HALF), jnp.bfloat16),
            pltpu.VMEM((2 * TOK, COLS), jnp.bfloat16),
            pltpu.VMEM((2, BLOCK, COLS), jnp.bfloat16),
            pltpu.SemaphoreType.DMA((2 * BLOCKS + 1,)),
        ],
        compiler_params=PARAMS,
        cost_estimate=cost(2 * 2 * TOK * HALF * COLS, 9 << 20),
        name="gradient_term",
    )(acts, got, grads, after)


def add_kernel(dims, n_outs, *refs):
    outs = refs[-n_outs:]
    for i, dim in enumerate(dims):
        keep, got = refs[2 * i : 2 * i + 2]
        blocks = keep.shape[0]
        inner = blocks >> (dim + 1)
        for slot in range(blocks):
            outs[2 * i + (slot // inner) % 2][slot // (2 * inner) * inner + slot % inner] = (
                keep[slot].astype(jnp.float32) + got[slot].astype(jnp.float32)
            ).astype(jnp.bfloat16)


def add_halves(pairs, dims, after=(), through=()):
    blocks = pairs[0].shape[0]
    half = jax.ShapeDtypeStruct((blocks // 2, ROWS, COLS), jnp.bfloat16)
    n, first = len(pairs), len(pairs) + len(after)
    return pl.pallas_call(
        functools.partial(add_kernel, dims, n + len(through)),
        out_shape=(half,) * n + tuple(jax.ShapeDtypeStruct(t.shape, t.dtype) for t in through),
        in_specs=[VMEM] * n + [ANY] * (len(after) + len(through)),
        out_specs=(VMEM,) * n + (ANY,) * len(through),
        input_output_aliases={first + i: n + i for i in range(len(through))},
        compiler_params=PARAMS,
        cost_estimate=cost(n * blocks << 15, n * blocks * 3 << 16),
        name="add_halves",
    )(*pairs, *after, *through)


def join_kernel(dim, here, got, both):
    blocks = here.shape[0]
    inner = blocks >> dim
    for slot in range(2 * blocks):
        source = got if (slot // inner) % 2 else here
        both[slot] = source[slot // (2 * inner) * inner + slot % inner]


def join(here, got, dim):
    blocks = here.shape[0]
    return pl.pallas_call(
        functools.partial(join_kernel, dim),
        out_shape=jax.ShapeDtypeStruct((2 * blocks, ROWS, COLS), jnp.bfloat16),
        in_specs=[VMEM, VMEM],
        out_specs=VMEM,
        compiler_params=PARAMS,
        cost_estimate=cost(0, blocks * 4 << 17),
        name="join",
    )(here, got)


STRIPE = 1024


def stage_kernel(tokens, got, *refs):
    both, sems = refs[-2:]
    where = place()
    run_all(
        [
            pltpu.make_async_copy(
                tokens.at[:, columns_of(where, r, where[4])],
                both.at[pl.ds(0, TOK), pl.ds(r * BLOCK, BLOCK)],
                sems.at[r],
            )
            for r in range(BLOCKS)
        ]
        + [pltpu.make_async_copy(got, both.at[pl.ds(TOK, TOK)], sems.at[BLOCKS])]
    )


def stage(tokens, got, after):
    return pl.pallas_call(
        stage_kernel,
        out_shape=jax.ShapeDtypeStruct((2 * TOK, HALF), jnp.bfloat16),
        in_specs=[ANY, ANY] + [VMEM] * len(after),
        out_specs=VMEM,
        scratch_shapes=[pltpu.SemaphoreType.DMA((BLOCKS + 1,))],
        compiler_params=PARAMS,
        cost_estimate=cost(0, 8 << 20),
        name="stage",
    )(tokens, got, *after)


def project_kernel(both, *refs):
    halves = refs[: 2 * PARTS]
    kept, mine, theirs, weights, total = refs[2 * PARTS :]
    where = place()
    per = STRIPE // BLOCK
    starts = [pair_starts(where, m) for m in range(PARTS)]

    def keep_block(x_hi, block):
        kept[pl.ds(pl.multiple_of(x_hi * BLOCK, BLOCK), BLOCK)] = block

    for s in range(HALF // STRIPE):
        for k in range(per):
            for m in range(PARTS):
                side, slot = side_and_slot(m, s * per + k)
                for j in range(2):
                    at = pl.ds(pl.multiple_of(k * BLOCK + starts[m][j], 32), 32)
                    weights[s % 2, at] = halves[2 * m + side][slot, j * 32 : j * 32 + 32]
        if s == 0:
            keep_block(where[0], weights[0, :BLOCK])

            @pl.when(where[4] == 1)
            def _():
                keep_block(1 - where[0], weights[0, 3 * BLOCK :])

        if s == 3:

            @pl.when(where[4] == 0)
            def _():
                keep_block(1 - where[0], weights[1, :BLOCK])

        product = jnp.dot(
            both[:, s * STRIPE : (s + 1) * STRIPE],
            weights[s % 2],
            preferred_element_type=jnp.float32,
        )
        if s == 0:
            total[...] = product
        elif s < HALF // STRIPE - 1:
            total[...] += product
        else:
            product += total[...]
            mine[...] = product[:TOK]
            theirs[...] = product[TOK:].astype(jnp.bfloat16)


def project(both, halves):
    return pl.pallas_call(
        project_kernel,
        out_shape=(
            jax.ShapeDtypeStruct((2 * BLOCK, COLS), jnp.bfloat16),
            jax.ShapeDtypeStruct((TOK, COLS), jnp.float32),
            jax.ShapeDtypeStruct((TOK, COLS), jnp.bfloat16),
        ),
        in_specs=[VMEM] * (1 + 2 * PARTS),
        out_specs=(VMEM,) * 3,
        scratch_shapes=[
            pltpu.VMEM((2, STRIPE, COLS), jnp.bfloat16),
            pltpu.VMEM((2 * TOK, COLS), jnp.float32),
        ],
        compiler_params=PARAMS,
        cost_estimate=cost(2 * 2 * TOK * HALF * COLS, 9 << 20),
        name="project",
    )(both, *halves)


def adamw_update(gradient, master_weights, first_moment, second_moment):
    new_first = beta_first * first_moment + (1.0 - beta_first) * gradient
    new_second = beta_second * second_moment + (1.0 - beta_second) * gradient * gradient
    first_hat = new_first / (1.0 - beta_first**ADAM_STEP)
    second_hat = new_second / (1.0 - beta_second**ADAM_STEP)
    new_master = master_weights - learn_rate * (
        first_hat / (jnp.sqrt(second_hat) + adam_eps) + decay_rate * master_weights
    )
    return (new_master, new_first, new_second)


def wide(array):
    return array.astype(jnp.float32)


def add(keep, got):
    return (wide(keep) + wide(got)).astype(jnp.bfloat16)


def halve(array, dim, pairing):
    keep = lax.index_in_dim(array, 0, dim, keepdims=False)
    return add(keep, across(lax.index_in_dim(array, 1, dim, keepdims=False), pairing))


def reduce_parts(halves, packed_tokens, state):
    pairs, dims = [], []
    for m, (v, w, _, _) in enumerate(ORDERS):
        pairs += [halves[2 * m], across(halves[2 * m + 1], v)]
        dims.append(w - (v < w))
    *sums, packed_tokens = add_halves(pairs, dims, (state,), (packed_tokens,))
    tokens = core_swap(packed_tokens)
    parts = []
    for m, (_, w, p, q) in enumerate(ORDERS):
        keep, send = sums[2 * m : 2 * m + 2]
        keep, send = add_halves([keep, across(send, w)], [int(p > q)])
        keep, send = add_halves([keep, across(send, p)], [0], () if m else (tokens,))
        total = wide(keep[0]) + wide(across(send[0], q))
        parts.append(total.astype(jnp.bfloat16) if m else total)
    return parts, tokens


def reduce_z(parts):
    total = parts[0]
    for m in range(1, PARTS):
        total = total + wide(z_swap(parts[m], m))
    total = total.astype(jnp.bfloat16)
    return (wide(total) + wide(z_swap(total, 7))).reshape(2, 32, COLS)


def gather_parts(rows):
    halves = []
    for m, (v, w, p, q) in enumerate(ORDERS):
        part = (z_swap(rows, m) if m else rows)[None]
        for bit, dim in ((q, 0), (p, sorted((p, q)).index(p)), (w, w - (v < w))):
            part = join(part, across(part, bit), dim)
        halves += [part, across(part, v)]
    return halves


def local(activations, output_grads, master_weights, first_moment, second_moment, next_tokens):
    low = lax.axis_index("outer") % 8 < 4
    packed, packed_acts = pack_acts(activations, output_grads)
    packed_tokens, state, packed_all = pack_rest(
        next_tokens, master_weights, first_moment, second_moment, packed_acts
    )
    halves = gradient_term(activations, core_swap(packed), output_grads, packed_all)
    got_state = z_swap(state, 7)

    parts, got_tokens = reduce_parts(halves, packed_tokens, got_state)
    gradient = reduce_z(parts)
    pairs = jnp.stack([jnp.where(low, state, got_state), jnp.where(low, got_state, state)], axis=1)
    updated = adamw_update(gradient, *pairs)
    new_master, new_first, new_second = (jnp.where(low, u[0], u[1]) for u in updated)
    rows = updated[0].astype(jnp.bfloat16).reshape(64, COLS)

    gathered = gather_parts(rows)
    both = stage(next_tokens, got_tokens, gathered[::2])
    kept_weights, mine, theirs = project(both, gathered)
    projection = (mine + wide(core_swap(theirs))).astype(jnp.bfloat16)
    return (new_master, new_first, new_second, kept_weights, projection)


def solution(mesh):
    placed = (
        P(("outer", "inner"), None),
        P(("outer", "inner"), None),
        P(("inner", "outer"), None),
        P(("inner", "outer"), None),
        P(("inner", "outer"), None),
        P(("outer", "inner"), None),
    )
    return jax.shard_map(
        local,
        mesh=mesh,
        in_specs=placed,
        out_specs=(
            P(("inner", "outer"), None),
            P(("inner", "outer"), None),
            P(("inner", "outer"), None),
            P("inner", None),
            P(("outer", "inner"), None),
        ),
        check_vma=False,
    )
```
